256 devices in a mesh: date: 32 (over y_hi, z, core), strip: 8 (over x, y_lo).
Axes of the slice: x: 4, y: 4 (y_hi: 2, y_lo: 2; y = y_hi * 2 + y_lo), z: 8, core: 2. Of those that a mesh axis runs over, the one named last changes fastest.
Arguments:
- slc: bfloat16 [64, 2, 320, 2560], P('date', None, 'strip')
- pair_second: int32 [64, 6], P('date'), may hold values from 0 to 63, as said below
- pair_count: int32 [64], P('date'), may hold values from 0 to 6, as said below
Outputs:
- interferogram: float32 [64, 6, 2, 64, 128], P('date', None, None, 'strip')
- coherence: float32 [64, 6, 64, 128], P('date', None, 'strip')
The draws below stay inside these ranges and needn't reach their ends.
Inputs may be any that keep to these rules, and one draw needn't show every extreme that they name: `pair_count`: date d has min(6, 63 - d, a drawn count of 2 to 6) pairs; date 0 has 6. For s < pair_count[d], pair_second[d, s] lies in d + 1 to d + 8, distinct within a date; the other slots hold d.
All inputs are finite; a program needn't handle non-finite values.
Results may differ from the reference program's by a relative error of at most 0.0003.
Values may be sent and summed in bfloat16 or wider, within the bound.
A program may use at most 64 MiB of HBM per device.

```python
import math
import jax
import jax.numpy as jnp
from jax import lax

RG = 2560
LOOK_AZ = 5
LOOK_RG = 20
WIN = 7
MAXOFF = 8
SLOTS = 6
DATES = 64
AZ = 320


def pair_tables(key):
    count_key, score_key = jax.random.split(jax.random.fold_in(key, 17))
    dates = jnp.arange(DATES, dtype=jnp.int32)
    avail = jnp.minimum(MAXOFF, DATES - 1 - dates)
    count = jnp.minimum(jax.random.randint(count_key, (DATES,), 2, SLOTS + 1), avail)
    count = jnp.where(dates == 0, SLOTS, count).astype(jnp.int32)
    offsets_all = jnp.arange(MAXOFF, dtype=jnp.int32)
    score = jax.random.randint(score_key, (DATES, MAXOFF), 0, 1 << 20) * 16 + offsets_all[None, :]
    score = jnp.where(offsets_all[None, :] + 1 > avail[:, None], score + (1 << 26), score)
    order = jnp.argsort(score, axis=1, stable=True).astype(jnp.int32)
    offsets = order[:, :SLOTS] + 1
    slot_ids = jnp.arange(SLOTS, dtype=jnp.int32)
    second = jnp.where(slot_ids[None, :] < count[:, None], dates[:, None] + offsets, dates[:, None])
    return (count, second.astype(jnp.int32))


def draw_pair_second(key, part):
    tables = pair_tables(key)
    return tables[1]


def draw_pair_count(key, part):
    tables = pair_tables(key)
    return tables[0]


def draw_slc(key, part):
    key = jax.random.fold_in(key, 5)
    keys = jax.random.split(key, 6)
    shape_full = (DATES, AZ // LOOK_AZ, LOOK_AZ, RG // LOOK_RG, LOOK_RG)
    shape_cell = (DATES, AZ // LOOK_AZ, 1, RG // LOOK_RG, 1)
    common_real = jax.random.normal(keys[0], (1,) + shape_full[1:], jnp.float32) * 0.7071
    common_imag = jax.random.normal(keys[1], (1,) + shape_full[1:], jnp.float32) * 0.7071
    corr = jax.random.uniform(keys[2], shape_cell, jnp.float32, 0.2, 0.95)
    phase = jax.random.uniform(keys[3], shape_cell, jnp.float32, -math.pi, math.pi)
    noise_real = jax.random.normal(keys[4], shape_full, jnp.float32) * 0.7071
    noise_imag = jax.random.normal(keys[5], shape_full, jnp.float32) * 0.7071
    rest = jnp.sqrt(1.0 - corr * corr)
    cosine = jnp.cos(phase)
    sine = jnp.sin(phase)
    part_real = corr * (common_real * cosine - common_imag * sine) + rest * noise_real
    part_imag = corr * (common_real * sine + common_imag * cosine) + rest * noise_imag
    stacked = jnp.stack([part_real, part_imag], 1)
    return stacked.reshape(DATES, 2, AZ, RG).astype(jnp.bfloat16)


def setup_inputs(seed: int = 0) -> dict:
    arg_keys = jax.random.split(jax.random.key(seed), 4)
    return {
        "slc": draw_slc(jax.random.fold_in(arg_keys[3], 71), 0),
        "pair_second": draw_pair_second(jax.random.fold_in(arg_keys[3], 71), 0),
        "pair_count": draw_pair_count(jax.random.fold_in(arg_keys[3], 71), 0),
    }


def multilook(field):
    shaped = field.reshape(field.shape[:-2] + (AZ // LOOK_AZ, LOOK_AZ, RG // LOOK_RG, LOOK_RG))
    return lax.optimization_barrier(jnp.sum(shaped, axis=(-3, -1))) / (LOOK_AZ * LOOK_RG)

def box_sum(field):
    half = WIN // 2
    rows = field.shape[-2]
    cols = field.shape[-1]
    widths = [(0, 0)] * (field.ndim - 2) + [(half, half), (half, half)]
    padded = jnp.pad(field, widths)
    across = padded[..., 0:rows, :]
    for shift_rows in range(1, WIN):
        across = across + padded[..., shift_rows:shift_rows + rows, :]
    total = across[..., 0:cols]
    for shift_cols in range(1, WIN):
        total = total + across[..., shift_cols:shift_cols + cols]
    return total

def reference(slc, pair_second, pair_count):

    def one_date(date):
        first = slc[date].astype(jnp.float32)
        second = slc[pair_second[date]].astype(jnp.float32)
        prod_real = first[0] * second[:, 0] + first[1] * second[:, 1]
        prod_imag = first[1] * second[:, 0] - first[0] * second[:, 1]
        power_sec = second[:, 0] * second[:, 0] + second[:, 1] * second[:, 1]
        power_ref = first[0] * first[0] + first[1] * first[1]
        look_real = multilook(prod_real)
        look_imag = multilook(prod_imag)
        look_sec = multilook(power_sec)
        look_ref = multilook(power_ref)
        box_real = box_sum(look_real)
        box_imag = box_sum(look_imag)
        box_sec = box_sum(look_sec)
        box_ref = box_sum(look_ref)[None]
        coher = jnp.sqrt(box_real * box_real + box_imag * box_imag) / jnp.sqrt(box_ref * box_sec)
        used = (jnp.arange(SLOTS) < pair_count[date])[:, None, None]
        ifg = jnp.stack([look_real, look_imag], 1)
        ifg = jnp.where(used[:, None], ifg, jnp.float32(0.0))
        coher = jnp.where(used, coher, jnp.float32(0.0))
        return (ifg, coher)
    interferogram, coherence = lax.map(one_date, jnp.arange(DATES, dtype=jnp.int32))
    return (interferogram, coherence)
```

```python
import jax
import jax.numpy as jnp
from jax import lax
from jax.experimental import pallas as pl
from jax.experimental.pallas import tpu as pltpu
from jax.sharding import PartitionSpec as P

MESH = pl.DeviceIdType.MESH
F32 = jnp.float32
BF16 = jnp.bfloat16

LOOK_AZ = 5
LOOK_RG = 20
SLOTS = 6
OFFS = 8
CHIPS = 16
STRIPS = 8
ROWS = 40
WIDTH = 2560
HALF = WIDTH // 2
LOOKS = ROWS // LOOK_AZ
CELLS = 128
PLANE_SCALE = 1.0 / (LOOK_AZ * LOOK_RG)

SAME = [(0, 1), (0, 2), (0, 3), (1, 2), (1, 3), (2, 3)]


def pair(a, b):
    return ("pair", a, b)


def power(a, b):
    return ("power", a, b)


STAGES = [
    [pair((0, a), (0, b)) for a, b in SAME] + [power((0, 0), (0, 1)), power((0, 2), (0, 3))],
    [pair((0, a), (1, 0)) for a in range(4)],
    [pair((0, a), (1, 1)) for a in range(4)] + [power((1, 0), (1, 1))],
    [pair((0, a), (1, 2)) for a in range(4)],
    [pair((0, a), (1, 3)) for a in range(4)] + [power((1, 2), (1, 3))],
]
STARTS = [0, 8, 12, 17, 21]
N_OWN = 26
IA, IB = 16, 25
BACK = [
    [],
    [(pair((-1, 3), (1, 0)), 0)],
    [(pair((-1, 3), (1, 1)), 1), (pair((-1, 2), (1, 0)), 2), (pair((-1, 2), (1, 1)), 3)],
    [(pair((-1, 3), (1, 2)), 4), (pair((-1, 2), (1, 2)), 5), (pair((-1, 1), (1, 0)), 9), (pair((-1, 1), (1, 1)), 10)],
    [(pair((-1, 3), (1, 3)), 7), (pair((-1, 0), (1, 0)), 12)],
]
BACK_IA, BACK_IB = (6, 11), (8, 13)
N_BACK = 14
BACK_SENDS = [(2, 1, 0, 4, 0), (3, 0, 9, 3, 4), (3, 1, 4, 3, 4), (4, 0, 12, 2, 7), (4, 1, 7, 2, 7)]
N_PLANES = N_OWN + 9


def kernel(slc, second, count, ifg, coh, tiles, looks, sums, table, res, back, lsem, xs, xr, us, ur, vs, vr, ps, pr, bs, br):
    date = lax.axis_index("date")
    strip = lax.axis_index("strip")
    q = date // 2
    c = date % 2
    other = 1 - c
    has_prev, has_next = q > 0, q < CHIPS - 1
    has_up, has_down = strip > 0, strip < STRIPS - 1

    def device(dq, core, ds):
        return ((q + dq) * 2 + core, strip + ds)

    def side_ok(ds):
        return {0: None, -1: has_up, 1: has_down}[ds]

    def chip_ok(dq):
        return {0: None, -1: has_prev, 1: has_next}[dq]

    def when(*conditions):
        conditions = [x for x in conditions if x is not None]
        if not conditions:
            return lambda f: f()
        total = conditions[0]
        for x in conditions[1:]:
            total = jnp.logical_and(total, x)
        return pl.when(total)

    barrier = pltpu.get_barrier_semaphore()
    pl.semaphore_signal(barrier, inc=1, device_id=device(0, other, 0), device_id_type=MESH)
    for dq in (-1, 1, 0):
        for ds in (0, -1, 1):
            if (dq, ds) == (0, 0):
                continue

            @when(chip_ok(dq), side_ok(ds))
            def _():
                for core in range(2):
                    pl.semaphore_signal(barrier, inc=1, device_id=device(dq, core, ds), device_id_type=MESH)

    own_copy = pltpu.make_async_copy(
        slc.at[:, :, :, pl.ds(pl.multiple_of(c * HALF, HALF), HALF)], tiles.at[1, pl.ds(2 * c, 2)], lsem
    )
    own_copy.start()

    first = lax.broadcasted_iota(jnp.int32, (CELLS, CELLS), 1) * LOOK_RG
    lane = lax.broadcasted_iota(jnp.int32, (CELLS, CELLS), 0)

    def fill(i, carry):
        delta = lane + i * CELLS - first
        inside = jnp.logical_and(delta >= 0, delta < LOOK_RG)
        table[pl.ds(pl.multiple_of(i * CELLS, CELLS), CELLS), :] = jnp.where(inside, 1.0, 0.0).astype(BF16)
        return carry

    lax.fori_loop(0, WIDTH // CELLS, fill, 0)
    row = lax.broadcasted_iota(jnp.int32, (ROWS, ROWS), 0)
    col = lax.broadcasted_iota(jnp.int32, (ROWS, ROWS), 1)
    order = jnp.where(col == LOOK_AZ * (row % LOOKS) + row // LOOKS, 1.0, 0.0).astype(BF16)

    @pl.when(jnp.logical_not(has_up))
    def _():
        res[0] = jnp.zeros(res.shape[1:], F32)

    @pl.when(jnp.logical_not(has_down))
    def _():
        res[2] = jnp.zeros(res.shape[1:], F32)

    def as_int(x):
        return jnp.where(x, 1, 0)

    chips = as_int(has_prev) + as_int(has_next)
    sides = as_int(has_up) + as_int(has_down)
    pl.semaphore_wait(barrier, 1 + 2 * chips + sides * (2 + 2 * chips))

    swap = pltpu.make_async_remote_copy(
        src_ref=slc.at[:, :, :, pl.ds(pl.multiple_of(other * HALF, HALF), HALF)],
        dst_ref=tiles.at[1, pl.ds(2 * c, 2)],
        send_sem=xs,
        recv_sem=xr,
        device_id=device(0, other, 0),
        device_id_type=MESH,
    )
    swap.start()

    def tile_copy(dq, j, core):
        send, recv = (us, ur) if dq < 0 else (vs, vr)
        return pltpu.make_async_remote_copy(
            src_ref=slc.at[j, :, :, pl.ds(core * HALF, HALF)],
            dst_ref=tiles.at[1 - dq, 2 * c + j],
            send_sem=send.at[j, core],
            recv_sem=recv.at[2 * c + j],
            device_id=device(dq, core, 0),
            device_id_type=MESH,
        )

    def send_tiles(dq, j):
        @pl.when(chip_ok(dq))
        def _():
            for core in range(2):
                tile_copy(dq, j, core).start()

    @pl.when(c == 0)
    def _():
        send_tiles(-1, 0)
        send_tiles(-1, 1)
        send_tiles(1, 1)
        send_tiles(1, 0)

    @pl.when(c == 1)
    def _():
        send_tiles(1, 1)
        send_tiles(1, 0)
        send_tiles(-1, 0)
        send_tiles(-1, 1)

    def wait_tile(rel, a):
        recv = ur if rel > 0 else vr

        @pl.when(chip_ok(rel))
        def _():
            pltpu.make_async_copy(tiles.at[1 + rel, a], tiles.at[1 + rel, a], recv.at[a]).wait()

    def reorder(rel, a):
        for part in range(2):
            looks[1 + rel, a, part] = jnp.dot(order, tiles[1 + rel, a, part], preferred_element_type=F32)

    def planes_of(stage):
        return STAGES[stage] + [p for p, _ in BACK[stage]]

    def compute(stage):
        planes = planes_of(stage)
        n = len(planes)

        def lanes(t, carry):
            at = pl.ds(pl.multiple_of(t * CELLS, CELLS), CELLS)
            at2 = pl.ds(pl.multiple_of(t * CELLS + HALF, CELLS), CELLS)

            def total(x):
                return jnp.sum(x.reshape(LOOK_AZ, LOOKS, CELLS), axis=0)

            for i, (kind, u, v) in enumerate(planes):
                ur_, ui_ = looks[1 + u[0], u[1], 0, :, at], looks[1 + u[0], u[1], 1, :, at]
                vr_, vi_ = looks[1 + v[0], v[1], 0, :, at], looks[1 + v[0], v[1], 1, :, at]
                if kind == "pair":
                    x, y = ur_ * vr_ + ui_ * vi_, ui_ * vr_ - ur_ * vi_
                else:
                    x, y = ur_ * ur_ + ui_ * ui_, vr_ * vr_ + vi_ * vi_
                sums[i, :, at] = total(x)
                sums[i, :, at2] = total(y)
            return carry

        lax.fori_loop(0, HALF // CELLS, lanes, 0)
        m = n + n % 2
        if m > n:
            sums[n] = jnp.zeros((LOOKS, WIDTH), F32)
        x = sums[0:m].reshape(m * LOOKS, WIDTH)
        hi = x.astype(BF16)
        lo = (x - hi.astype(F32)).astype(BF16)
        t = table[...]
        out = jnp.dot(hi, t, preferred_element_type=F32) + jnp.dot(lo, t, preferred_element_type=F32)
        out = (out * PLANE_SCALE).reshape(m, LOOKS, CELLS)
        own = len(STAGES[stage])
        res[1, c, STARTS[stage] : STARTS[stage] + own] = out[0:own]
        for i, (_, place) in enumerate(BACK[stage]):
            back[place] = out[own + i]
        if stage == 2:
            for place in BACK_IA:
                back[place] = out[own - 1]
        if stage == 4:
            for place in BACK_IB:
                back[place] = out[own - 1]

    def own_send(stage, target, ds):
        span = pl.ds(STARTS[stage], len(STAGES[stage]))
        k = target if ds != 0 else 2
        return pltpu.make_async_remote_copy(
            src_ref=res.at[1, c, span],
            dst_ref=res.at[1 - ds, c, span],
            send_sem=ps.at[stage, 1 + ds, k],
            recv_sem=pr.at[stage, 1 - ds, c],
            device_id=device(0, other if ds == 0 else target, ds),
            device_id_type=MESH,
        )

    def back_send(m, ds):
        _, core, start, size, place = BACK_SENDS[m]
        return pltpu.make_async_remote_copy(
            src_ref=back.at[pl.ds(start, size)],
            dst_ref=res.at[1 - ds, c, pl.ds(N_OWN + place, size)],
            send_sem=bs.at[m, 1 + ds],
            recv_sem=br.at[m, 1 - ds, c],
            device_id=device(-1, core, ds),
            device_id_type=MESH,
        )

    def all_sends(stage, act):
        for m, spec in enumerate(BACK_SENDS):
            if spec[0] == stage:
                for ds in (0, -1, 1):

                    @when(has_prev, side_ok(ds))
                    def _():
                        act(back_send(m, ds))

        for ds in (-1, 1):

            @when(side_ok(ds))
            def _():
                for target in range(2):
                    act(own_send(stage, target, ds))

        act(own_send(stage, 2, 0))

    own_copy.wait()
    swap.wait_recv()
    for a in range(4):
        reorder(0, a)
    compute(0)
    all_sends(0, lambda copy: copy.start())
    for stage in range(1, 5):
        b, a = stage - 1, 4 - stage
        wait_tile(1, b)
        reorder(1, b)
        wait_tile(-1, a)
        reorder(-1, a)
        compute(stage)
        all_sends(stage, lambda copy: copy.start())

    for stage in range(5):
        span = pl.ds(STARTS[stage], len(STAGES[stage]))
        for ds in (0, -1, 1):
            for h in range(2):
                alive = h != c if ds == 0 else side_ok(ds)

                @pl.when(alive)
                def _():
                    ref = res.at[1 + ds, h, span]
                    pltpu.make_async_copy(ref, ref, pr.at[stage, 1 + ds, h]).wait()

    for m, (_, core, _, size, place) in enumerate(BACK_SENDS):
        for ds in (0, -1, 1):

            @when(has_next, c == core, side_ok(ds))
            def _():
                for h in range(2):
                    ref = res.at[1 + ds, h, pl.ds(N_OWN + place, size)]
                    pltpu.make_async_copy(ref, ref, br.at[m, 1 + ds, h]).wait()

    sub = lax.broadcasted_iota(jnp.int32, (LOOKS, CELLS), 0)
    lane8 = lax.broadcasted_iota(jnp.int32, (LOOKS, CELLS), 1)
    left = lane8 < CELLS // 2

    def rows_box(plane, h):
        before, here, after = res[0, h, plane], res[1, h, plane], res[2, h, plane]
        total = here
        for k in range(1, 4):
            total = total + pltpu.roll(jnp.where(sub >= LOOKS - k, before, here), k, 0)
            total = total + pltpu.roll(jnp.where(sub < k, after, here), LOOKS - k, 0)
        return total

    def low(p0, p1):
        return jnp.where(left, p0, pltpu.roll(p1, CELLS // 2, 1))

    def high(p0, p1):
        return jnp.where(left, pltpu.roll(p0, CELLS // 2, 1), p1)

    def cells_box(x):
        total = x
        for k in range(1, 4):
            total = total + jnp.where(lane8 >= k, pltpu.roll(x, k, 1), 0.0)
            total = total + jnp.where(lane8 < CELLS - k, pltpu.roll(x, CELLS - k, 1), 0.0)
        return total

    for j in range(2):
        a = 2 * c + j
        p = jnp.where(c == 0, 6, 7)
        r0, r1 = rows_box(p, 0), rows_box(p, 1)
        box_ref = cells_box(low(r0, r1) if j == 0 else high(r0, r1))
        for s in range(SLOTS):
            e = second[j, s]
            used = s < count[j]
            off = jnp.clip(e - (4 * q + a), 1, OFFS)
            b = jnp.where(off <= 3 - a, 0, jnp.where(off <= 7 - a, off - (4 - a), off - (8 - a)))
            base = jnp.where(a == 0, 0, jnp.where(a == 1, 3, 5))
            same = base + off - 1
            following = 8 + 4 * b + a + jnp.where(b >= 2, 1, 0)
            far3 = jnp.where(b < 2, b, jnp.where(b == 2, 4, 7))
            far2 = jnp.where(b < 2, 2 + b, 5)
            far = N_OWN + jnp.where(a == 3, far3, jnp.where(a == 2, far2, jnp.where(a == 1, 4 + b, 7)))
            near = off <= 3 - a
            middle = off <= 7 - a
            plane = jnp.where(near, same, jnp.where(middle, following, far))
            e4 = lax.rem(a + off, 4)
            later = e4 >= 2
            sec_near = jnp.where(later, 7, 6)
            sec_mid = jnp.where(later, IB, IA)
            sec_far = N_OWN + jnp.where(later, 8, 6)
            plane_sec = jnp.where(near, sec_near, jnp.where(middle, sec_mid, sec_far))
            odd = lax.rem(a + off, 2) == 1
            p0, p1 = res[1, 0, plane], res[1, 1, plane]
            zero = jnp.zeros((LOOKS, CELLS), F32)
            ifg[j, s, 0] = jnp.where(used, low(p0, p1), zero)
            ifg[j, s, 1] = jnp.where(used, high(p0, p1), zero)
            b0, b1 = rows_box(plane, 0), rows_box(plane, 1)
            s0, s1 = rows_box(plane_sec, 0), rows_box(plane_sec, 1)
            box_r, box_i = cells_box(low(b0, b1)), cells_box(high(b0, b1))
            box_s = cells_box(jnp.where(odd, high(s0, s1), low(s0, s1)))
            value = jnp.sqrt(box_r * box_r + box_i * box_i) / jnp.sqrt(box_ref * box_s)
            coh[j, s] = jnp.where(used, value, zero)

    swap.wait_send()
    for dq in (-1, 1):

        @pl.when(chip_ok(dq))
        def _():
            for j in range(2):
                for core in range(2):
                    tile_copy(dq, j, core).wait_send()

    for stage in range(5):
        all_sends(stage, lambda copy: copy.wait_send())


def shards(slc, pair_second, pair_count):
    dma = pltpu.SemaphoreType.DMA
    hbm = pl.BlockSpec(memory_space=pl.ANY)
    smem = pl.BlockSpec(memory_space=pltpu.SMEM)
    vmem = pl.BlockSpec(memory_space=pltpu.VMEM)
    return pl.pallas_call(
        kernel,
        out_shape=(
            jax.ShapeDtypeStruct((2, SLOTS, 2, LOOKS, CELLS), F32),
            jax.ShapeDtypeStruct((2, SLOTS, LOOKS, CELLS), F32),
        ),
        in_specs=[hbm, smem, smem],
        out_specs=(vmem, vmem),
        scratch_shapes=[
            pltpu.VMEM((3, 4, 2, ROWS, HALF), BF16),
            pltpu.VMEM((3, 4, 2, ROWS, HALF), F32),
            pltpu.VMEM((8, LOOKS, WIDTH), F32),
            pltpu.VMEM((WIDTH, CELLS), BF16),
            pltpu.VMEM((3, 2, N_PLANES, LOOKS, CELLS), F32),
            pltpu.VMEM((N_BACK, LOOKS, CELLS), F32),
            dma,
            dma,
            dma,
            dma((2, 2)),
            dma((4,)),
            dma((2, 2)),
            dma((4,)),
            dma((5, 3, 3)),
            dma((5, 3, 2)),
            dma((5, 3)),
            dma((5, 3, 2)),
        ],
        compiler_params=pltpu.CompilerParams(
            collective_id=0, has_side_effects=True, vmem_limit_bytes=40 * 2**20
        ),
    )(slc, pair_second, pair_count)


def solution(mesh):
    in_specs = (P("date", None, "strip", None), P("date", None), P("date"))
    out_specs = (P("date", None, None, "strip", None), P("date", None, "strip", None))
    return jax.shard_map(shards, mesh=mesh, in_specs=in_specs, out_specs=out_specs, check_vma=False)
```

```python
import jax
import jax.numpy as jnp
from jax import lax
from jax.experimental import pallas as pl
from jax.experimental.pallas import tpu as pltpu
from jax.sharding import PartitionSpec as P

MESH = pl.DeviceIdType.MESH
F32 = jnp.float32
BF16 = jnp.bfloat16

LOOK_AZ = 5
LOOK_RG = 20
SLOTS = 6
OFFS = 8
CHIPS = 16
STRIPS = 8
ROWS = 40
WIDTH = 2560
HALF = WIDTH // 2
LOOKS = ROWS // LOOK_AZ
CELLS = 128
PLANE_SCALE = 1.0 / (LOOK_AZ * LOOK_RG)


def pair(a, b):
    return ("pair", a, b)


def power(a, b):
    return ("power", a, b)


def onto(b, *middle):
    return [pair((0, 0), (1, b)), pair((0, 1), (1, b)), *middle, pair((0, 2), (1, b)), pair((0, 3), (1, b))]


NEXT = [(0, 2), (2, 0), (1, 3), (3, 1)]
PREV = [(1, 3), (3, 1), (0, 2), (2, 0)]
SAME = [(0, 1), (0, 2), (0, 3), (1, 2), (1, 3)]
STAGES = [
    [pair((0, a), (0, b)) for a, b in SAME] + [power((0, 0), (0, 2)), power((0, 1), (0, 3)), pair((0, 2), (0, 3))],
    onto(NEXT[0]),
    onto(NEXT[1], power((1, 0), (1, 2))),
    onto(NEXT[2]),
    onto(NEXT[3], power((1, 1), (1, 3))),
]
STARTS = [0, 8, 12, 17, 21]
NEEDS = [[(0, 7), (5, 3)], [(0, 2), (2, 2)], [(0, 3), (2, 3)], [(0, 2), (2, 2)], [(0, 3), (2, 3)]]
N_OWN = 26
BACK = [
    [],
    [(((1, 0), 0), ((3, 2), 2))],
    [(((3, 0), 4), ((3, 0), 3)), (((3, 2), 5), ((1, 0), 0))],
    [(((0, 0), 1), ((3, 3), 4)), (((1, 1), 2), ((2, 0), 5)), (((3, 1), 6), ((2, 2), 6))],
    [(((2, 0), 10), ((3, 1), 12)), (((2, 2), 11), ((2, 1), 13)), (((2, 1), 12), ((1, 1), 9)), (((3, 3), 13), ((0, 0), 10))],
]
BACK_POWER = {2: [(3, 7), (1, 7)], 4: [(8, 9), (8, 11)]}
N_BACK = 14
BACK_SENDS = [
    (3, 0, 0, 0, 4),
    (3, 0, 1, 4, 4),
    (3, 1, 0, 0, 2),
    (3, 1, 1, 2, 6),
    (4, 0, 0, 8, 1),
    (4, 0, 1, 9, 5),
    (4, 1, 0, 8, 3),
    (4, 1, 1, 11, 3),
]
FAR = [{}, {}]
for stage_ in BACK:
    for both_ in stage_:
        for core_ in range(2):
            FAR[core_][both_[core_][0]] = both_[core_][1]
N_PLANES = N_OWN + N_BACK


def when(*conditions):
    conditions = [x for x in conditions if x is not None]
    if not conditions:
        return lambda f: f()
    total = conditions[0]
    for x in conditions[1:]:
        total = jnp.logical_and(total, x)
    return pl.when(total)


def planes_kernel(
    slc, second_in, count_in, ifg, coh, res, edge, tiles, looks, sums, table, back, rim, back_rim, second, count,
    lsem, sem2, xs, xr, us, ur, vs, vr, fs, ps, pr, hs, hr, bs, br,
):
    date = lax.axis_index("date")
    strip = lax.axis_index("strip")
    q = date // 2
    c = date % 2
    other = 1 - c
    has_prev, has_next = q > 0, q < CHIPS - 1
    has_up, has_down = strip > 0, strip < STRIPS - 1

    def device(dq, core, ds):
        return ((q + dq) * 2 + core, strip + ds)

    def side_ok(ds):
        return {0: None, -1: has_up, 1: has_down}[ds]

    def chip_ok(dq):
        return {0: None, -1: has_prev, 1: has_next}[dq]

    def by_core(x):
        if isinstance(x, tuple):
            return jnp.where(c == 0, x[0], x[1])
        return x

    own_copy = pltpu.make_async_copy(
        slc.at[:, :, :, pl.ds(pl.multiple_of(c * HALF, HALF), HALF)], tiles.at[1, pl.ds(2 * c, 2)], lsem
    )
    own_copy.start()
    second_copy = pltpu.make_async_copy(second_in, second, sem2.at[0])
    count_copy = pltpu.make_async_copy(count_in, count, sem2.at[1])
    second_copy.start()
    count_copy.start()

    barrier = pltpu.get_barrier_semaphore()
    for dq in (-1, 1):

        @when(chip_ok(dq))
        def _():
            for core in range(2):
                pl.semaphore_signal(barrier, inc=1, device_id=device(dq, core, 0), device_id_type=MESH)

    pl.semaphore_signal(barrier, inc=1, device_id=device(0, other, 0), device_id_type=MESH)
    for ds in (-1, 1):

        @when(side_ok(ds))
        def _():
            pl.semaphore_signal(barrier, inc=1, device_id=device(0, c, ds), device_id_type=MESH)

    last, mid = CHIPS - 1, CHIPS // 2

    def hello(chip, cores):
        for core in cores:
            pl.semaphore_signal(barrier, inc=1, device_id=(chip * 2 + core, strip), device_id_type=MESH)

    pl.when(q == 0)(lambda: hello(mid, (0, 1)))
    pl.when(q == mid - 1)(lambda: hello(0, (c,)))
    pl.when(q == last)(lambda: hello(mid - 1, (0, 1)))
    pl.when(q == mid)(lambda: hello(last, (c,)))

    def as_int(x):
        return jnp.where(x, 1, 0)

    relays = jnp.logical_or(q == 0, q == last)
    relayed = jnp.logical_or(q == mid - 1, q == mid)
    greeted = 1 + 2 * (as_int(has_prev) + as_int(has_next)) + as_int(has_up) + as_int(has_down)
    pl.semaphore_wait(barrier, greeted + as_int(relays) + 2 * as_int(relayed))

    swap = pltpu.make_async_remote_copy(
        src_ref=slc.at[:, :, :, pl.ds(pl.multiple_of(other * HALF, HALF), HALF)],
        dst_ref=tiles.at[1, pl.ds(2 * c, 2)],
        send_sem=xs,
        recv_sem=xr,
        device_id=device(0, other, 0),
        device_id_type=MESH,
    )

    def tile_copy(dq, j, core, relay):
        send, recv = (us, ur) if dq < 0 else (vs, vr)
        chip = q + dq
        if relay:
            chip = 0 if dq < 0 else last
        if relay:
            recv = vr if dq < 0 else ur
        return pltpu.make_async_remote_copy(
            src_ref=slc.at[j, :, :, pl.ds(core * HALF, HALF)],
            dst_ref=tiles.at[1 + dq if relay else 1 - dq, 2 * c + j],
            send_sem=send.at[j, core],
            recv_sem=recv.at[2 * c + j],
            device_id=(chip * 2 + core, strip),
            device_id_type=MESH,
        )

    def forward_copy(a, side, recv, chip, step):
        return pltpu.make_async_remote_copy(
            src_ref=tiles.at[2 - side, a],
            dst_ref=tiles.at[side, a],
            send_sem=fs.at[step],
            recv_sem=recv.at[a],
            device_id=(chip * 2 + c, strip),
            device_id_type=MESH,
        )

    def pass_on(step):
        def one(a, side, came, recv, chip):
            pltpu.make_async_copy(tiles.at[2 - side, a], tiles.at[2 - side, a], came.at[a]).wait()
            forward_copy(a, side, recv, chip, step).start()

        pl.when(q == 0)(lambda: one(by_core(NEXT[2 + step]), 2, vr, ur, mid - 1))
        pl.when(q == last)(lambda: one(by_core(PREV[2 + step]), 0, ur, vr, mid))

    def passed_on(step):
        pl.when(q == 0)(lambda: forward_copy(by_core(NEXT[2 + step]), 2, ur, mid - 1, step).wait_send())
        pl.when(q == last)(lambda: forward_copy(by_core(PREV[2 + step]), 0, vr, mid, step).wait_send())

    def tile_sends(act):
        for here in range(2):

            @pl.when(c == here)
            def _():
                for n in range(4):
                    for dq in (-1, 1):
                        j = n // 2 if dq < 0 else 1 - n // 2
                        core = (here + n) % 2

                        far = q == (mid if dq < 0 else mid - 1)
                        if n < 2:
                            when(chip_ok(dq))(lambda: act(tile_copy(dq, j, core, False)))
                        else:
                            when(chip_ok(dq), jnp.logical_not(far))(lambda: act(tile_copy(dq, j, core, False)))
                            when(far)(lambda: act(tile_copy(dq, j, core, True)))

    def start(copy):
        copy.start()

    def wait_send(copy):
        copy.wait_send()

    swap.start()
    tile_sends(start)

    first = lax.broadcasted_iota(jnp.int32, (CELLS, CELLS), 1) * LOOK_RG
    lane = lax.broadcasted_iota(jnp.int32, (CELLS, CELLS), 0)

    def fill(i, carry):
        delta = lane + i * CELLS - first
        inside = jnp.logical_and(delta >= 0, delta < LOOK_RG)
        table[pl.ds(pl.multiple_of(i * CELLS, CELLS), CELLS), :] = jnp.where(inside, 1.0, 0.0).astype(BF16)
        return carry

    lax.fori_loop(0, WIDTH // CELLS, fill, 0)
    row = lax.broadcasted_iota(jnp.int32, (ROWS, ROWS), 0)
    col = lax.broadcasted_iota(jnp.int32, (ROWS, ROWS), 1)
    order = jnp.where(col == LOOK_AZ * (row % LOOKS) + row // LOOKS, 1.0, 0.0).astype(BF16)
    sub = lax.broadcasted_iota(jnp.int32, (LOOKS, CELLS), 0)
    lane8 = lax.broadcasted_iota(jnp.int32, (LOOKS, CELLS), 1)
    left = lane8 < CELLS // 2

    @pl.when(jnp.logical_not(has_up))
    def _():
        edge[0] = jnp.zeros(edge.shape[1:], F32)

    @pl.when(jnp.logical_not(has_down))
    def _():
        edge[1] = jnp.zeros(edge.shape[1:], F32)

    def wait_tile(rel, a):
        recv = ur if rel > 0 else vr

        @when(chip_ok(rel))
        def _():
            pltpu.make_async_copy(tiles.at[1 + rel, a], tiles.at[1 + rel, a], recv.at[a]).wait()

    def reorder(rel, a):
        @when(chip_ok(rel))
        def _():
            for part in range(2):
                looks[1 + rel, a, part] = jnp.dot(order, tiles[1 + rel, a, part], preferred_element_type=F32)

    def rims(x):
        d = jnp.where(sub < 3, pltpu.roll(x, 3, 0), 0.0)
        d = d + pltpu.roll(d, LOOKS - 1, 0) + pltpu.roll(d, LOOKS - 2, 0)
        u = jnp.where(jnp.logical_and(sub >= 1, sub < 4), pltpu.roll(x, 1, 0), 0.0)
        u = u + pltpu.roll(u, 1, 0) + pltpu.roll(u, 2, 0)
        return d[0:4], u[0:4]

    def compute(stage):
        planes = list(STAGES[stage])
        for (pair0, _), (pair1, _) in BACK[stage]:
            planes.append(pair((-1, (pair0[0], pair1[0])), (1, (pair0[1], pair1[1]))))
        planes = [(kind, (u[0], by_core(u[1])), (v[0], by_core(v[1]))) for kind, u, v in planes]
        n = len(planes)

        def lanes(t, carry):
            at = pl.ds(pl.multiple_of(t * CELLS, CELLS), CELLS)
            at2 = pl.ds(pl.multiple_of(t * CELLS + HALF, CELLS), CELLS)

            def total(x):
                return jnp.sum(x.reshape(LOOK_AZ, LOOKS, CELLS), axis=0)

            for i, (kind, u, v) in enumerate(planes):
                u_r, u_i = looks[1 + u[0], u[1], 0, :, at], looks[1 + u[0], u[1], 1, :, at]
                v_r, v_i = looks[1 + v[0], v[1], 0, :, at], looks[1 + v[0], v[1], 1, :, at]
                if kind == "pair":
                    x, y = u_r * v_r + u_i * v_i, u_i * v_r - u_r * v_i
                else:
                    x, y = u_r * u_r + u_i * u_i, v_r * v_r + v_i * v_i
                sums[i, :, at] = total(x)
                sums[i, :, at2] = total(y)
            return carry

        lax.fori_loop(0, HALF // CELLS, lanes, 0)
        m = n + n % 2
        if m > n:
            sums[n] = jnp.zeros((LOOKS, WIDTH), F32)
        x = sums[0:m].reshape(m * LOOKS, WIDTH)
        hi = x.astype(BF16)
        lo = (x - hi.astype(F32)).astype(BF16)
        t = table[...]
        out = jnp.dot(hi, t, preferred_element_type=F32) + jnp.dot(lo, t, preferred_element_type=F32)
        out = (out * PLANE_SCALE).reshape(m, LOOKS, CELLS)
        own = len(STAGES[stage])
        for i in range(own):
            res[c, STARTS[stage] + i] = out[i]
            rim[0, STARTS[stage] + i], rim[1, STARTS[stage] + i] = rims(out[i])
        places = [(own + i, (p0, p1)) for i, ((_, p0), (_, p1)) in enumerate(BACK[stage])]
        if stage in BACK_POWER:
            places += [(2, (p0, p1)) for p0, p1 in zip(*BACK_POWER[stage], strict=True)]
        for i, place in places:
            place = by_core(place)
            back[place] = out[i]
            back_rim[0, place], back_rim[1, place] = rims(out[i])

    def span_of(stage, core):
        if stage == 0:
            return pl.ds(0, 8)
        return pl.ds(STARTS[stage] + 2 * core, NEEDS[stage][0][1])

    def core_send(stage):
        return pltpu.make_async_remote_copy(
            src_ref=res.at[c, span_of(stage, other)],
            dst_ref=res.at[c, span_of(stage, other)],
            send_sem=ps.at[stage],
            recv_sem=pr.at[stage],
            device_id=device(0, other, 0),
            device_id_type=MESH,
        )

    def rim_send(stage, core, ds):
        first_, size = NEEDS[stage][core]
        side = (1 - ds) // 2
        span = pl.ds(STARTS[stage] + first_, size)
        return pltpu.make_async_remote_copy(
            src_ref=rim.at[side, span],
            dst_ref=edge.at[side, c, span],
            send_sem=hs.at[stage, core, side],
            recv_sem=hr.at[stage, c, side],
            device_id=device(0, core, ds),
            device_id_type=MESH,
        )

    def back_send(m, ds):
        _, _, core, first_, size = BACK_SENDS[m]
        span, there = pl.ds(first_, size), pl.ds(N_OWN + first_, size)
        if ds == 0:
            src, dst = back.at[span], res.at[c, there]
        else:
            side = (1 - ds) // 2
            src, dst = back_rim.at[side, span], edge.at[side, c, there]
        return pltpu.make_async_remote_copy(
            src_ref=src,
            dst_ref=dst,
            send_sem=bs.at[m, 1 + ds],
            recv_sem=br.at[m, 1 + ds],
            device_id=device(-1, core, ds),
            device_id_type=MESH,
        )

    def all_sends(stage, act):
        for here in range(2):
            specs = [m for m, spec in enumerate(BACK_SENDS) if spec[0] == stage and spec[1] == here]
            if specs:

                @when(c == here, has_prev)
                def _():
                    for ds in (-1, 1, 0):

                        @when(side_ok(ds))
                        def _():
                            for m in specs:
                                act(back_send(m, ds))

        for ds in (-1, 1):

            @when(side_ok(ds))
            def _():
                for core in range(2):
                    act(rim_send(stage, core, ds))

        act(core_send(stage))

    def own_arrivals(stage):
        ref = res.at[other, span_of(stage, c)]
        pltpu.make_async_copy(ref, ref, pr.at[stage]).wait()
        for ds in (-1, 1):
            side = (1 - ds) // 2
            for core in range(2):
                first_, size = NEEDS[stage][core]

                @when(side_ok(-ds), c == core)
                def _():
                    for h in range(2):
                        ref = edge.at[side, h, pl.ds(STARTS[stage] + first_, size)]
                        pltpu.make_async_copy(ref, ref, hr.at[stage, h, side]).wait()

    def back_arrivals(stage):
        for core in range(2):
            for ds in (0, -1, 1):

                @when(has_next, c == core, side_ok(-ds))
                def _():
                    for m, (after, h, to, first_, size) in enumerate(BACK_SENDS):
                        if after == stage and to == core:
                            span = pl.ds(N_OWN + first_, size)
                            ref = res.at[h, span] if ds == 0 else edge.at[(1 - ds) // 2, h, span]
                            pltpu.make_async_copy(ref, ref, br.at[m, 1 + ds]).wait()

    own_copy.wait()
    second_copy.wait()
    count_copy.wait()
    swap.wait_recv()
    for a in range(4):
        reorder(0, a)
    compute(0)
    all_sends(0, start)
    swap.wait_send()
    for stage in range(1, 5):
        b, a = by_core(NEXT[stage - 1]), by_core(PREV[stage - 1])
        wait_tile(1, b)
        reorder(1, b)
        wait_tile(-1, a)
        reorder(-1, a)
        compute(stage)
        all_sends(stage, start)
        if stage <= 2:
            pass_on(stage - 1)
        all_sends(stage - 1, wait_send)
        own_arrivals(stage - 1)
    tile_sends(wait_send)
    for step in range(2):
        passed_on(step)
    back_arrivals(3)
    own_arrivals(4)
    back_arrivals(4)

    def low(p0, p1):
        return jnp.where(left, p0, pltpu.roll(p1, CELLS // 2, 1))

    def high(p0, p1):
        return jnp.where(left, pltpu.roll(p0, CELLS // 2, 1), p1)

    def rows_box(h, plane):
        x = res[h, plane]
        total = x + jnp.concatenate([edge[0, h, plane], edge[1, h, plane]], axis=0)
        for k in range(1, 4):
            total = total + jnp.where(sub >= k, pltpu.roll(x, k, 0), 0.0)
            total = total + jnp.where(sub < LOOKS - k, pltpu.roll(x, LOOKS - k, 0), 0.0)
        return total

    def cells_box(x):
        total = x
        for k in range(1, 4):
            total = total + jnp.where(lane8 >= k, pltpu.roll(x, k, 1), 0.0)
            total = total + jnp.where(lane8 < CELLS - k, pltpu.roll(x, CELLS - k, 1), 0.0)
        return total

    def table_of(a, b, entries):
        value = 0
        for (ea, eb), place in entries.items():
            value = jnp.where(jnp.logical_and(a == ea, b == eb), place, value)
        return value

    zero = jnp.zeros((LOOKS, CELLS), F32)
    for j in range(2):
        a = 2 * c + j
        p = 5 + j
        r0, r1 = rows_box(0, p), rows_box(1, p)
        box_ref = cells_box(jnp.where(c == 0, low(r0, r1), high(r0, r1)))
        for s in range(SLOTS):
            used = s < count[j]
            off = jnp.clip(second[j, s] - (4 * q + a), 1, OFFS)
            near, middle = off <= 3 - a, off <= 7 - a
            e = lax.rem(a + off, 4)
            same = off - 1 + jnp.where(a == 0, 0, jnp.where(a == 1, 3, 7))
            planes, secs = [], []
            for h in range(2):
                here = e if h == 0 else jnp.where(e >= 2, e - 2, e + 2)
                step = jnp.where(here == 1, 2, jnp.where(here == 2, 1, here))
                up = jnp.where(jnp.logical_and(lax.rem(step, 2) == 1, a >= 2), 1, 0)
                following = 8 + 4 * step + jnp.where(step >= 2, 1, 0) + a + up
                far = N_OWN + table_of(a, e, FAR[h])
                planes.append(jnp.where(near, same, jnp.where(middle, following, far)))
                power2 = BACK_POWER[2][h]
                power4 = BACK_POWER[4][h]
                far_even = N_OWN + jnp.where(c == 0, power2[0], power2[1])
                far_odd = N_OWN + jnp.where(c == 0, power4[0], power4[1])
                sec_even = jnp.where(near, 5, jnp.where(middle, 14, far_even))
                sec_odd = jnp.where(near, 6, jnp.where(middle, 23, far_odd))
                secs.append(jnp.where(lax.rem(e, 2) == 1, sec_odd, sec_even))
            p0, p1 = res[0, planes[0]], res[1, planes[1]]
            ifg[j, s, 0] = jnp.where(used, low(p0, p1), zero)
            ifg[j, s, 1] = jnp.where(used, high(p0, p1), zero)
            b0, b1 = rows_box(0, planes[0]), rows_box(1, planes[1])
            s0, s1 = rows_box(0, secs[0]), rows_box(1, secs[1])
            box_r, box_i = cells_box(low(b0, b1)), cells_box(high(b0, b1))
            box_s = cells_box(jnp.where(e >= 2, high(s0, s1), low(s0, s1)))
            value = jnp.sqrt(box_r * box_r + box_i * box_i) / jnp.sqrt(box_ref * box_s)
            coh[j, s] = jnp.where(used, value, zero)

    all_sends(4, wait_send)


def store_kernel(ifg, coh, ifg_out, coh_out, sems):
    copies = [
        pltpu.make_async_copy(ifg, ifg_out, sems.at[0]),
        pltpu.make_async_copy(coh, coh_out, sems.at[1]),
    ]
    for copy in copies:
        copy.start()
    for copy in copies:
        copy.wait()


def shards(slc, pair_second, pair_count):
    dma = pltpu.SemaphoreType.DMA
    hbm = pl.BlockSpec(memory_space=pltpu.HBM)
    vmem = pl.BlockSpec(memory_space=pltpu.VMEM)
    ifg_shape = (2, SLOTS, 2, LOOKS, CELLS)
    coh_shape = (2, SLOTS, LOOKS, CELLS)
    operands = [pltpu.with_memory_space_constraint(x, pltpu.HBM) for x in (slc, pair_second, pair_count)]
    ifg, coh = pl.pallas_call(
        planes_kernel,
        out_shape=(pltpu.VMEM(ifg_shape, F32), pltpu.VMEM(coh_shape, F32)),
        in_specs=[hbm, hbm, hbm],
        out_specs=(vmem, vmem),
        scratch_shapes=[
            pltpu.VMEM((2, N_PLANES, LOOKS, CELLS), F32),
            pltpu.VMEM((2, 2, N_PLANES, 4, CELLS), F32),
            pltpu.VMEM((3, 4, 2, ROWS, HALF), BF16),
            pltpu.VMEM((3, 4, 2, ROWS, HALF), F32),
            pltpu.VMEM((10, LOOKS, WIDTH), F32),
            pltpu.VMEM((WIDTH, CELLS), BF16),
            pltpu.VMEM((N_BACK, LOOKS, CELLS), F32),
            pltpu.VMEM((2, N_OWN, 4, CELLS), F32),
            pltpu.VMEM((2, N_BACK, 4, CELLS), F32),
            pltpu.SMEM((2, SLOTS), jnp.int32),
            pltpu.SMEM((2,), jnp.int32),
            dma,
            dma((2,)),
            dma,
            dma,
            dma((2, 2)),
            dma((4,)),
            dma((2, 2)),
            dma((4,)),
            dma((2,)),
            dma((5,)),
            dma((5,)),
            dma((5, 2, 2)),
            dma((5, 2, 2)),
            dma((8, 3)),
            dma((8, 3)),
        ],
        compiler_params=pltpu.CompilerParams(
            collective_id=0, has_side_effects=True, vmem_limit_bytes=40 * 2**20
        ),
    )(*operands)
    return pl.pallas_call(
        store_kernel,
        out_shape=(jax.ShapeDtypeStruct(ifg_shape, F32), jax.ShapeDtypeStruct(coh_shape, F32)),
        in_specs=[vmem, vmem],
        out_specs=(pl.BlockSpec(memory_space=pl.ANY), pl.BlockSpec(memory_space=pl.ANY)),
        scratch_shapes=[dma((2,))],
        compiler_params=pltpu.CompilerParams(vmem_limit_bytes=16 * 2**20),
    )(ifg, coh)


def solution(mesh):
    in_specs = (P("date", None, "strip", None), P("date", None), P("date"))
    out_specs = (P("date", None, None, "strip", None), P("date", None, "strip", None))
    return jax.shard_map(shards, mesh=mesh, in_specs=in_specs, out_specs=out_specs, check_vma=False)
```

```python
import jax
import jax.numpy as jnp
from jax import lax
from jax.experimental import pallas as pl
from jax.experimental.pallas import tpu as pltpu
from jax.sharding import PartitionSpec as P

MESH = pl.DeviceIdType.MESH
F32 = jnp.float32
BF16 = jnp.bfloat16

LOOK_AZ = 5
LOOK_RG = 20
SLOTS = 6
OFFS = 8
CHIPS = 16
STRIPS = 8
ROWS = 40
WIDTH = 2560
HALF = WIDTH // 2
LOOKS = ROWS // LOOK_AZ
CELLS = 128
PLANE_SCALE = 1.0 / (LOOK_AZ * LOOK_RG)


def pair(a, b):
    return ("pair", a, b)


def power(a, b):
    return ("power", a, b)


def onto(b, *middle):
    return [pair((0, 0), (1, b)), pair((0, 1), (1, b)), *middle, pair((0, 2), (1, b)), pair((0, 3), (1, b))]


NEXT = [(0, 2), (2, 0), (1, 3), (3, 1)]
PREV = [(1, 3), (3, 1), (0, 2), (2, 0)]
SAME = [(0, 1), (0, 2), (0, 3), (1, 2), (1, 3)]
STAGES = [
    [pair((0, a), (0, b)) for a, b in SAME] + [power((0, 0), (0, 2)), power((0, 1), (0, 3)), pair((0, 2), (0, 3))],
    onto(NEXT[0]),
    onto(NEXT[1], power((1, 0), (1, 2))),
    onto(NEXT[2]),
    onto(NEXT[3], power((1, 1), (1, 3))),
]
STARTS = [0, 8, 12, 17, 21]
NEEDS = [[(0, 7), (5, 3)], [(0, 2), (2, 2)], [(0, 3), (2, 3)], [(0, 2), (2, 2)], [(0, 3), (2, 3)]]
N_OWN = 26
IA, IB = 14, 23
BACK = [
    [],
    [(((1, 0), 0), ((3, 2), 2))],
    [(((3, 0), 4), ((3, 0), 3)), (((3, 2), 5), ((1, 0), 0))],
    [(((0, 0), 1), ((3, 3), 4)), (((1, 1), 2), ((2, 0), 5)), (((3, 1), 6), ((2, 2), 6))],
    [(((2, 0), 10), ((3, 1), 12)), (((2, 2), 11), ((2, 1), 13)), (((2, 1), 12), ((1, 1), 9)), (((3, 3), 13), ((0, 0), 10))],
]
BACK_POWER = {2: [(3, 7), (1, 7)], 4: [(8, 9), (8, 11)]}
N_BACK = 14
BACK_SENDS = [
    (3, 0, 0, 0, 4),
    (3, 0, 1, 4, 4),
    (3, 1, 0, 0, 2),
    (3, 1, 1, 2, 6),
    (4, 0, 0, 8, 1),
    (4, 0, 1, 9, 5),
    (4, 1, 0, 8, 3),
    (4, 1, 1, 11, 3),
]
FAR = [{}, {}]
for stage_ in BACK:
    for both_ in stage_:
        for core_ in range(2):
            FAR[core_][both_[core_][0]] = both_[core_][1]
N_PLANES = N_OWN + N_BACK


def arrival(b, core):
    return 1 + [x[core] for x in NEXT].index(b)


def finals(core, when_):
    found = []
    for j in range(2):
        a = 2 * core + j
        for off in range(1, OFFS + 1):
            chip, e = divmod(a + off, 4)
            odd, half = e % 2, e // 2
            if chip == 0:
                step, place = 0, [(SAME + [None, None, (2, 3)]).index((a, e))] * 2
                sec = [6 if odd else 5] * 2
            elif chip == 1:
                step, place = 2 if odd else 1, []
                for h in range(2):
                    t = arrival(e, h)
                    place.append(STARTS[t] + a + (1 if t % 2 == 0 and a >= 2 else 0))
                sec = [IB if odd else IA] * 2
            else:
                place = [N_OWN + FAR[h][(a, e)] for h in range(2)]
                late = any(spec[0] == 4 and spec[1] == h and spec[3] <= FAR[h][(a, e)] < spec[3] + spec[4] for spec in BACK_SENDS for h in range(2))
                step = 4 if late or odd else 3
                sec = [N_OWN + BACK_POWER[4 if odd else 2][h][core] for h in range(2)]
            if step == when_:
                found.append((j, off, place, sec, half))
    return found


def when(*conditions):
    conditions = [x for x in conditions if x is not None]
    if not conditions:
        return lambda f: f()
    total = conditions[0]
    for x in conditions[1:]:
        total = jnp.logical_and(total, x)
    return pl.when(total)


def planes_kernel(
    slc, second_in, count_in, ifg, coh, res, edge, tiles, looks, sums, table, back, rim, back_rim, second, count, every_ifg, every_coh, box_ref,
    lsem, sem2, xs, xr, us, ur, vs, vr, us2, ur2, vs2, vr2, fs, ps, pr, hs, hr, bs, br,
):
    date = lax.axis_index("date")
    strip = lax.axis_index("strip")
    q = date // 2
    c = date % 2
    other = 1 - c
    has_prev, has_next = q > 0, q < CHIPS - 1
    has_up, has_down = strip > 0, strip < STRIPS - 1

    def device(dq, core, ds):
        return ((q + dq) * 2 + core, strip + ds)

    def side_ok(ds):
        return {0: None, -1: has_up, 1: has_down}[ds]

    def chip_ok(dq):
        return {0: None, -1: has_prev, 1: has_next}[dq]

    def by_core(x):
        if isinstance(x, tuple):
            return jnp.where(c == 0, x[0], x[1])
        return x

    own_copy = pltpu.make_async_copy(
        slc.at[:, :, :, pl.ds(pl.multiple_of(c * HALF, HALF), HALF)], tiles.at[1, pl.ds(2 * c, 2)], lsem
    )
    own_copy.start()
    second_copy = pltpu.make_async_copy(second_in, second, sem2.at[0])
    count_copy = pltpu.make_async_copy(count_in, count, sem2.at[1])
    second_copy.start()
    count_copy.start()

    barrier = pltpu.get_barrier_semaphore()
    for dq in (-1, 1):

        @when(chip_ok(dq))
        def _():
            for core in range(2):
                pl.semaphore_signal(barrier, inc=1, device_id=device(dq, core, 0), device_id_type=MESH)

    pl.semaphore_signal(barrier, inc=1, device_id=device(0, other, 0), device_id_type=MESH)
    for ds in (-1, 1):

        @when(side_ok(ds))
        def _():
            pl.semaphore_signal(barrier, inc=1, device_id=device(0, c, ds), device_id_type=MESH)

    last, mid = CHIPS - 1, CHIPS // 2

    def hello(chip, cores):
        for core in cores:
            pl.semaphore_signal(barrier, inc=1, device_id=(chip * 2 + core, strip), device_id_type=MESH)

    pl.when(q == 0)(lambda: hello(mid, (0, 1)))
    pl.when(q == mid - 1)(lambda: hello(0, (c,)))
    pl.when(q == last)(lambda: hello(mid - 1, (0, 1)))
    pl.when(q == mid)(lambda: hello(last, (c,)))

    def as_int(x):
        return jnp.where(x, 1, 0)

    relays = jnp.logical_or(q == 0, q == last)
    relayed = jnp.logical_or(q == mid - 1, q == mid)
    greeted = 1 + 2 * (as_int(has_prev) + as_int(has_next)) + as_int(has_up) + as_int(has_down)
    pl.semaphore_wait(barrier, greeted + as_int(relays) + 2 * as_int(relayed))

    swap = pltpu.make_async_remote_copy(
        src_ref=slc.at[:, :, :, pl.ds(pl.multiple_of(other * HALF, HALF), HALF)],
        dst_ref=tiles.at[1, pl.ds(2 * c, 2)],
        send_sem=xs,
        recv_sem=xr,
        device_id=device(0, other, 0),
        device_id_type=MESH,
    )

    def tile_copy(dq, j, core, relay, part):
        send, recv = (us.at[j, core], ur) if dq < 0 else (vs.at[j, core], vr)
        if part == 1:
            send = us2 if dq < 0 else vs2
        chip = q + dq
        if relay:
            chip = 0 if dq < 0 else last
        if relay:
            recv = vr if dq < 0 else ur
        if part == 1:
            recv = {0: ur2, 1: vr2}[0 if recv is ur else 1]
        start_, width = (0, HALF) if part is None else (part * HALF // 2, HALF // 2)
        return pltpu.make_async_remote_copy(
            src_ref=slc.at[j, :, :, pl.ds(core * HALF + start_, width)],
            dst_ref=tiles.at[1 + dq if relay else 1 - dq, 2 * c + j, :, :, pl.ds(start_, width)],
            send_sem=send,
            recv_sem=recv.at[2 * c + j],
            device_id=(chip * 2 + core, strip),
            device_id_type=MESH,
        )

    PARTS = [(0, None), (1, 0), (1, 1)]

    def part_of(ref, part):
        if part is None:
            return ref
        return ref.at[:, :, pl.ds(part * HALF // 2, HALF // 2)]

    def forward_copy(n, at_first):
        step, part = PARTS[n]
        a = by_core((NEXT if at_first else PREV)[2 + step])
        side = 2 if at_first else 0
        came, recv = (vr, ur) if at_first else (ur, vr)
        if part == 1:
            came, recv = (vr2, ur2) if at_first else (ur2, vr2)
        here = part_of(tiles.at[2 - side, a], part)
        copy = pltpu.make_async_remote_copy(
            src_ref=here,
            dst_ref=part_of(tiles.at[side, a], part),
            send_sem=fs.at[n],
            recv_sem=recv.at[a],
            device_id=((mid - 1 if at_first else mid) * 2 + c, strip),
            device_id_type=MESH,
        )
        return here, came.at[a], copy

    def pass_on(n):
        def one(at_first):
            here, came, copy = forward_copy(n, at_first)
            pltpu.make_async_copy(here, here, came).wait()
            copy.start()

        pl.when(q == 0)(lambda: one(True))
        pl.when(q == last)(lambda: one(False))

    def passed_on(n):
        pl.when(q == 0)(lambda: forward_copy(n, True)[2].wait_send())
        pl.when(q == last)(lambda: forward_copy(n, False)[2].wait_send())

    def tile_sends(act):
        for here in range(2):

            @pl.when(c == here)
            def _():
                for n in range(4):
                    for dq in (-1, 1):
                        j = n // 2 if dq < 0 else 1 - n // 2
                        core = (here + n) % 2

                        far = q == (mid if dq < 0 else mid - 1)

                        def send_parts(relay):
                            for part in (0, 1) if n == 3 else (None,):
                                act(tile_copy(dq, j, core, relay, part))

                        if n < 2:
                            when(chip_ok(dq))(lambda: send_parts(False))
                        else:
                            when(chip_ok(dq), jnp.logical_not(far))(lambda: send_parts(False))
                            when(far)(lambda: send_parts(True))

    def start(copy):
        copy.start()

    def wait_send(copy):
        copy.wait_send()

    swap.start()
    tile_sends(start)

    first = lax.broadcasted_iota(jnp.int32, (CELLS, CELLS), 1) * LOOK_RG
    lane = lax.broadcasted_iota(jnp.int32, (CELLS, CELLS), 0)

    def fill(i, carry):
        delta = lane + i * CELLS - first
        inside = jnp.logical_and(delta >= 0, delta < LOOK_RG)
        table[pl.ds(pl.multiple_of(i * CELLS, CELLS), CELLS), :] = jnp.where(inside, 1.0, 0.0).astype(BF16)
        return carry

    lax.fori_loop(0, WIDTH // CELLS, fill, 0)
    row = lax.broadcasted_iota(jnp.int32, (ROWS, ROWS), 0)
    col = lax.broadcasted_iota(jnp.int32, (ROWS, ROWS), 1)
    order = jnp.where(col == LOOK_AZ * (row % LOOKS) + row // LOOKS, 1.0, 0.0).astype(BF16)
    sub = lax.broadcasted_iota(jnp.int32, (LOOKS, CELLS), 0)
    lane8 = lax.broadcasted_iota(jnp.int32, (LOOKS, CELLS), 1)
    left = lane8 < CELLS // 2

    @pl.when(jnp.logical_not(has_up))
    def _():
        edge[0] = jnp.zeros(edge.shape[1:], F32)

    @pl.when(jnp.logical_not(has_down))
    def _():
        edge[1] = jnp.zeros(edge.shape[1:], F32)

    def get_tile(rel, a, part):
        @when(chip_ok(rel))
        def _():
            whole, second_half = (ur, ur2) if rel > 0 else (vr, vr2)
            ref = part_of(tiles.at[1 + rel, a], part)
            pltpu.make_async_copy(ref, ref, (second_half if part == 1 else whole).at[a]).wait()
            reorder(rel, a, part)

    def reorder(rel, a, part):
        at = slice(None) if part is None else pl.ds(part * HALF // 2, HALF // 2)
        for i in range(2):
            looks[1 + rel, a, i, :, at] = jnp.dot(order, tiles[1 + rel, a, i, :, at], preferred_element_type=F32)

    def rims(x):
        d = jnp.where(sub < 3, pltpu.roll(x, 3, 0), 0.0)
        d = d + pltpu.roll(d, LOOKS - 1, 0) + pltpu.roll(d, LOOKS - 2, 0)
        u = jnp.where(jnp.logical_and(sub >= 1, sub < 4), pltpu.roll(x, 1, 0), 0.0)
        u = u + pltpu.roll(u, 1, 0) + pltpu.roll(u, 2, 0)
        return d[0:4], u[0:4]

    def planes_of(stage, own, far):
        planes = list(STAGES[stage]) if own else []
        if far:
            for (pair0, _), (pair1, _) in BACK[stage]:
                planes.append(pair((-1, (pair0[0], pair1[0])), (1, (pair0[1], pair1[1]))))
        return [(kind, (u[0], by_core(u[1])), (v[0], by_core(v[1]))) for kind, u, v in planes]

    def looked(planes, at0, part):
        n = len(planes)
        m = n + n % 2

        def lanes(t, carry):
            at = pl.ds(pl.multiple_of(t * CELLS, CELLS), CELLS)
            at2 = pl.ds(pl.multiple_of(t * CELLS + HALF, CELLS), CELLS)

            def total(x):
                return jnp.sum(x.reshape(LOOK_AZ, LOOKS, CELLS), axis=0)

            for i, (kind, u, v) in enumerate(planes):
                u_r, u_i = looks[1 + u[0], u[1], 0, :, at], looks[1 + u[0], u[1], 1, :, at]
                v_r, v_i = looks[1 + v[0], v[1], 0, :, at], looks[1 + v[0], v[1], 1, :, at]
                if kind == "pair":
                    x, y = u_r * v_r + u_i * v_i, u_i * v_r - u_r * v_i
                else:
                    x, y = u_r * u_r + u_i * u_i, v_r * v_r + v_i * v_i
                sums[at0 + i, :, at] = total(x)
                sums[at0 + i, :, at2] = total(y)
            return carry

        steps = HALF // CELLS
        spans = [(0, WIDTH)]
        first_, end = 0, steps
        if part is not None:
            spans = [(part * HALF // 2, HALF // 2), (HALF + part * HALF // 2, HALF // 2)]
            first_, end = part * steps // 2, (part + 1) * steps // 2
        lax.fori_loop(first_, end, lanes, 0)
        if m > n:
            sums[at0 + n] = jnp.zeros((LOOKS, WIDTH), F32)
        out = None
        for at, width in spans:
            x = sums[at0 : at0 + m, :, at : at + width].reshape(m * LOOKS, width)
            hi = x.astype(BF16)
            lo = (x - hi.astype(F32)).astype(BF16)
            t = table[at : at + width, :]
            y = jnp.dot(hi, t, preferred_element_type=F32) + jnp.dot(lo, t, preferred_element_type=F32)
            out = y if out is None else out + y
        return out

    def as_planes(out):
        return (out * PLANE_SCALE).reshape(out.shape[0] // LOOKS, LOOKS, CELLS)

    def put_back(places, out):
        for i, place in places:
            place = by_core(place)
            back[place] = out[i]
            back_rim[0, place], back_rim[1, place] = rims(out[i])

    def put_own(stage, out):
        for i in range(len(STAGES[stage])):
            res[c, STARTS[stage] + i] = out[i]
            rim[0, STARTS[stage] + i], rim[1, STARTS[stage] + i] = rims(out[i])
        if stage in BACK_POWER:
            put_back([(2, both) for both in zip(*BACK_POWER[stage], strict=True)], out)

    def put_far(stage, out):
        put_back([(i, (p0, p1)) for i, ((_, p0), (_, p1)) in enumerate(BACK[stage])], out)

    def compute(stage):
        out = as_planes(looked(planes_of(stage, True, True), 0, None))
        put_own(stage, out)
        put_far(stage, out[len(STAGES[stage]) :])

    def span_of(stage, core):
        if stage == 0:
            return pl.ds(0, 8)
        return pl.ds(STARTS[stage] + 2 * core, NEEDS[stage][0][1])

    def core_send(stage):
        return pltpu.make_async_remote_copy(
            src_ref=res.at[c, span_of(stage, other)],
            dst_ref=res.at[c, span_of(stage, other)],
            send_sem=ps.at[stage],
            recv_sem=pr.at[stage],
            device_id=device(0, other, 0),
            device_id_type=MESH,
        )

    def rim_send(stage, core, ds):
        first_, size = NEEDS[stage][core]
        side = (1 - ds) // 2
        span = pl.ds(STARTS[stage] + first_, size)
        return pltpu.make_async_remote_copy(
            src_ref=rim.at[side, span],
            dst_ref=edge.at[side, c, span],
            send_sem=hs.at[stage, core, side],
            recv_sem=hr.at[stage],
            device_id=device(0, core, ds),
            device_id_type=MESH,
        )

    def back_send(m, ds):
        _, _, core, first_, size = BACK_SENDS[m]
        span, there = pl.ds(first_, size), pl.ds(N_OWN + first_, size)
        if ds == 0:
            src, dst = back.at[span], res.at[c, there]
        else:
            side = (1 - ds) // 2
            src, dst = back_rim.at[side, span], edge.at[side, c, there]
        return pltpu.make_async_remote_copy(
            src_ref=src,
            dst_ref=dst,
            send_sem=bs.at[m, 1 + ds],
            recv_sem=br.at[m, 0 if ds == 0 else 1],
            device_id=device(-1, core, ds),
            device_id_type=MESH,
        )

    def back_sends(stage, act):
        for here in range(2):
            specs = [m for m, spec in enumerate(BACK_SENDS) if spec[0] == stage and spec[1] == here]
            if specs:

                @when(c == here, has_prev)
                def _():
                    for ds in (-1, 1, 0):

                        @when(side_ok(ds))
                        def _():
                            for m in specs:
                                act(back_send(m, ds))

    def own_sends(stage, act):
        for ds in (-1, 1):

            @when(side_ok(ds))
            def _():
                for core in range(2):
                    act(rim_send(stage, core, ds))

        act(core_send(stage))

    def all_sends(stage, act):
        back_sends(stage, act)
        own_sends(stage, act)

    def wait_for(ref, sem):
        pltpu.make_async_copy(ref, ref, sem).wait()

    def edge_wait(h, span, sem):
        here = edge if h is None else edge.at[:, pl.ds(h, 1)]
        when(has_up, has_down)(lambda: wait_for(here.at[:, :, span], sem))
        when(jnp.logical_not(has_up))(lambda: wait_for(here.at[1, :, span], sem))
        when(jnp.logical_not(has_down))(lambda: wait_for(here.at[0, :, span], sem))

    def own_arrivals(stage):
        wait_for(res.at[other, span_of(stage, c)], pr.at[stage])
        if stage == 0:
            for core in range(2):
                first_, size = NEEDS[0][core]
                pl.when(c == core)(lambda: edge_wait(None, pl.ds(first_, size), hr.at[0]))
        else:
            edge_wait(None, span_of(stage, c), hr.at[stage])

    def back_arrivals(stage):
        for core in range(2):

            @when(has_next, c == core)
            def _():
                for m, (after, h, to, first_, size) in enumerate(BACK_SENDS):
                    if after == stage and to == core:
                        span = pl.ds(N_OWN + first_, size)
                        wait_for(res.at[h, span], br.at[m, 0])
                        edge_wait(h, span, br.at[m, 1])

    def low(p0, p1):
        return jnp.where(left, p0, pltpu.roll(p1, CELLS // 2, 1))

    def high(p0, p1):
        return jnp.where(left, pltpu.roll(p0, CELLS // 2, 1), p1)

    def rows_box(h, plane):
        x = res[h, plane]
        total = x + jnp.concatenate([edge[0, h, plane], edge[1, h, plane]], axis=0)
        for k in range(1, 4):
            total = total + jnp.where(sub >= k, pltpu.roll(x, k, 0), 0.0)
            total = total + jnp.where(sub < LOOKS - k, pltpu.roll(x, LOOKS - k, 0), 0.0)
        return total

    def cells_box(x):
        total = x
        for k in range(1, 4):
            total = total + jnp.where(lane8 >= k, pltpu.roll(x, k, 1), 0.0)
            total = total + jnp.where(lane8 < CELLS - k, pltpu.roll(x, CELLS - k, 1), 0.0)
        return total

    def ref_boxes():
        for j in range(2):
            r0, r1 = rows_box(0, 5 + j), rows_box(1, 5 + j)
            box_ref[j] = cells_box(jnp.where(c == 0, low(r0, r1), high(r0, r1)))

    def coherences(step):
        for core in range(2):

            @pl.when(c == core)
            def _():
                for j, off, place, sec, half in finals(core, step):
                    p0, p1 = res[0, place[0]], res[1, place[1]]
                    every_ifg[j, off - 1, 0] = low(p0, p1)
                    every_ifg[j, off - 1, 1] = high(p0, p1)
                    b0, b1 = rows_box(0, place[0]), rows_box(1, place[1])
                    s0, s1 = rows_box(0, sec[0]), rows_box(1, sec[1])
                    box_r, box_i = cells_box(low(b0, b1)), cells_box(high(b0, b1))
                    box_s = cells_box(high(s0, s1) if half else low(s0, s1))
                    top = jnp.sqrt(box_r * box_r + box_i * box_i)
                    every_coh[j, off - 1] = top / jnp.sqrt(box_ref[j] * box_s)

    own_copy.wait()
    second_copy.wait()
    count_copy.wait()
    chosen = []
    for j in range(2):
        for slot in range(SLOTS):
            off = jnp.clip(second[j, slot] - (4 * q + 2 * c + j), 1, OFFS)
            chosen.append((j, slot, off - 1, slot < count[j]))
    swap.wait_recv()
    for a in range(4):
        reorder(0, a, None)
    compute(0)
    all_sends(0, start)
    swap.wait_send()
    for stage in range(1, 5):
        b, a = by_core(NEXT[stage - 1]), by_core(PREV[stage - 1])
        if stage < 4:
            get_tile(1, b, None)
            get_tile(-1, a, None)
            compute(stage)
            all_sends(stage, start)
        else:
            own, far = planes_of(4, True, False), planes_of(4, False, True)
            get_tile(1, b, 0)
            own_out = looked(own, 0, 0)
            get_tile(-1, a, 0)
            far_out = looked(far, 6, 0)
            get_tile(1, b, 1)
            put_own(4, as_planes(own_out + looked(own, 0, 1)))
            own_sends(4, start)
            get_tile(-1, a, 1)
            put_far(4, as_planes(far_out + looked(far, 6, 1)))
            back_sends(4, start)
        if stage == 1:
            pass_on(0)
        if stage == 2:
            pass_on(1)
            pass_on(2)
        all_sends(stage - 1, wait_send)
        own_arrivals(stage - 1)
        if stage == 1:
            ref_boxes()
            coherences(0)
        if stage == 3:
            coherences(1)
    tile_sends(wait_send)
    for n in range(3):
        passed_on(n)
    own_arrivals(4)
    coherences(2)
    back_arrivals(3)
    coherences(3)
    back_arrivals(4)
    coherences(4)

    zero = jnp.zeros((LOOKS, CELLS), F32)
    for j, slot, off, used in chosen:
        for part in range(2):
            ifg[j, slot, part] = jnp.where(used, every_ifg[j, off, part], zero)
        coh[j, slot] = jnp.where(used, every_coh[j, off], zero)

    all_sends(4, wait_send)


def store_kernel(ifg, coh, ifg_out, coh_out, sems):
    copies = [
        pltpu.make_async_copy(ifg, ifg_out, sems.at[0]),
        pltpu.make_async_copy(coh, coh_out, sems.at[1]),
    ]
    for copy in copies:
        copy.start()
    for copy in copies:
        copy.wait()


def shards(slc, pair_second, pair_count):
    dma = pltpu.SemaphoreType.DMA
    hbm = pl.BlockSpec(memory_space=pltpu.HBM)
    vmem = pl.BlockSpec(memory_space=pltpu.VMEM)
    ifg_shape = (2, SLOTS, 2, LOOKS, CELLS)
    coh_shape = (2, SLOTS, LOOKS, CELLS)
    operands = [pltpu.with_memory_space_constraint(x, pltpu.HBM) for x in (slc, pair_second, pair_count)]
    ifg, coh = pl.pallas_call(
        planes_kernel,
        out_shape=(pltpu.VMEM(ifg_shape, F32), pltpu.VMEM(coh_shape, F32)),
        in_specs=[hbm, hbm, hbm],
        out_specs=(vmem, vmem),
        scratch_shapes=[
            pltpu.VMEM((2, N_PLANES, LOOKS, CELLS), F32),
            pltpu.VMEM((2, 2, N_PLANES, 4, CELLS), F32),
            pltpu.VMEM((3, 4, 2, ROWS, HALF), BF16),
            pltpu.VMEM((3, 4, 2, ROWS, HALF), F32),
            pltpu.VMEM((10, LOOKS, WIDTH), F32),
            pltpu.VMEM((WIDTH, CELLS), BF16),
            pltpu.VMEM((N_BACK, LOOKS, CELLS), F32),
            pltpu.VMEM((2, N_OWN, 4, CELLS), F32),
            pltpu.VMEM((2, N_BACK, 4, CELLS), F32),
            pltpu.SMEM((2, SLOTS), jnp.int32),
            pltpu.SMEM((2,), jnp.int32),
            pltpu.VMEM((2, OFFS, 2, LOOKS, CELLS), F32),
            pltpu.VMEM((2, OFFS, LOOKS, CELLS), F32),
            pltpu.VMEM((2, LOOKS, CELLS), F32),
            dma,
            dma((2,)),
            dma,
            dma,
            dma((2, 2)),
            dma((4,)),
            dma((2, 2)),
            dma((4,)),
            dma,
            dma((4,)),
            dma,
            dma((4,)),
            dma((3,)),
            dma((5,)),
            dma((5,)),
            dma((5, 2, 2)),
            dma((5,)),
            dma((8, 3)),
            dma((8, 2)),
        ],
        compiler_params=pltpu.CompilerParams(
            collective_id=0, has_side_effects=True, vmem_limit_bytes=40 * 2**20
        ),
    )(*operands)
    return pl.pallas_call(
        store_kernel,
        out_shape=(jax.ShapeDtypeStruct(ifg_shape, F32), jax.ShapeDtypeStruct(coh_shape, F32)),
        in_specs=[vmem, vmem],
        out_specs=(pl.BlockSpec(memory_space=pl.ANY), pl.BlockSpec(memory_space=pl.ANY)),
        scratch_shapes=[dma((2,))],
        compiler_params=pltpu.CompilerParams(vmem_limit_bytes=16 * 2**20),
    )(ifg, coh)


def solution(mesh):
    in_specs = (P("date", None, "strip", None), P("date", None), P("date"))
    out_specs = (P("date", None, None, "strip", None), P("date", None, "strip", None))
    return jax.shard_map(shards, mesh=mesh, in_specs=in_specs, out_specs=out_specs, check_vma=False)
```

```python
import jax
import jax.numpy as jnp
from jax import lax
from jax.experimental import pallas as pl
from jax.experimental.pallas import tpu as pltpu
from jax.sharding import PartitionSpec as P

MESH = pl.DeviceIdType.MESH
F32 = jnp.float32
BF16 = jnp.bfloat16

LOOK_AZ = 5
LOOK_RG = 20
SLOTS = 6
OFFS = 8
CHIPS = 16
STRIPS = 8
ROWS = 40
WIDTH = 2560
HALF = WIDTH // 2
LOOKS = ROWS // LOOK_AZ
CELLS = 128
PLANE_SCALE = 1.0 / (LOOK_AZ * LOOK_RG)


def pair(a, b):
    return ("pair", a, b)


def power(a, b):
    return ("power", a, b)


def onto(b, *middle):
    return [pair((0, 0), (1, b)), pair((0, 1), (1, b)), *middle, pair((0, 2), (1, b)), pair((0, 3), (1, b))]


NEXT = [(0, 2), (2, 0), (1, 3), (3, 1)]
PREV = [(1, 3), (3, 1), (0, 2), (2, 0)]
SAME = [(0, 1), (0, 2), (0, 3), (1, 2), (1, 3)]
STAGES = [
    [pair((0, a), (0, b)) for a, b in SAME] + [power((0, 0), (0, 2)), power((0, 1), (0, 3)), pair((0, 2), (0, 3))],
    onto(NEXT[0]),
    onto(NEXT[1], power((1, 0), (1, 2))),
    onto(NEXT[2]),
    onto(NEXT[3], power((1, 1), (1, 3))),
]
STARTS = [0, 8, 12, 17, 21]
NEEDS = [[(0, 7), (5, 3)], [(0, 2), (2, 2)], [(0, 3), (2, 3)], [(0, 2), (2, 2)], [(0, 3), (2, 3)]]
N_OWN = 26
IA, IB = 14, 23
BACK = [
    [],
    [(((1, 0), 0), ((3, 2), 2))],
    [(((3, 0), 4), ((3, 0), 3)), (((3, 2), 5), ((1, 0), 0))],
    [(((0, 0), 1), ((3, 3), 4)), (((1, 1), 2), ((2, 0), 5)), (((3, 1), 6), ((2, 2), 6))],
    [(((2, 0), 10), ((3, 1), 12)), (((2, 2), 11), ((2, 1), 13)), (((2, 1), 12), ((1, 1), 9)), (((3, 3), 13), ((0, 0), 10))],
]
BACK_POWER = {2: [(3, 7), (1, 7)], 4: [(8, 9), (8, 11)]}
N_BACK = 14
BACK_SENDS = [
    (3, 0, 0, 0, 4),
    (3, 0, 1, 4, 4),
    (3, 1, 0, 0, 2),
    (3, 1, 1, 2, 6),
    (4, 0, 0, 8, 1),
    (4, 0, 1, 9, 5),
    (4, 1, 0, 8, 3),
    (4, 1, 1, 11, 3),
]
FAR = [{}, {}]
for stage_ in BACK:
    for both_ in stage_:
        for core_ in range(2):
            FAR[core_][both_[core_][0]] = both_[core_][1]
N_PLANES = N_OWN + N_BACK


def arrival(b, core):
    return 1 + [x[core] for x in NEXT].index(b)


def finals(core, when_):
    found = []
    for j in range(2):
        a = 2 * core + j
        for off in range(1, OFFS + 1):
            chip, e = divmod(a + off, 4)
            odd, half = e % 2, e // 2
            if chip == 0:
                step, place = 0, [(SAME + [None, None, (2, 3)]).index((a, e))] * 2
                sec = [6 if odd else 5] * 2
            elif chip == 1:
                step, place = 2 if odd else 1, []
                for h in range(2):
                    t = arrival(e, h)
                    place.append(STARTS[t] + a + (1 if t % 2 == 0 and a >= 2 else 0))
                sec = [IB if odd else IA] * 2
            else:
                place = [N_OWN + FAR[h][(a, e)] for h in range(2)]
                late = any(spec[0] == 4 and spec[1] == h and spec[3] <= FAR[h][(a, e)] < spec[3] + spec[4] for spec in BACK_SENDS for h in range(2))
                step = 4 if late or odd else 3
                sec = [N_OWN + BACK_POWER[4 if odd else 2][h][core] for h in range(2)]
            if step == when_:
                found.append((j, off, place, sec, half))
    return found


def when(*conditions):
    conditions = [x for x in conditions if x is not None]
    if not conditions:
        return lambda f: f()
    total = conditions[0]
    for x in conditions[1:]:
        total = jnp.logical_and(total, x)
    return pl.when(total)


def planes_kernel(
    slc, second_in, count_in, ifg, coh, res, edge, tiles, looks, sums, table, back, rim, back_rim, second, count, every_ifg, every_coh, box_ref,
    ready, lsem, sem2, xs, xr, us, ur, vs, vr, us2, ur2, vs2, vr2, fs, ps, pr, hs, hr, bs, br,
):
    date = lax.axis_index("date")
    strip = lax.axis_index("strip")
    q = date // 2
    c = date % 2
    other = 1 - c
    has_prev, has_next = q > 0, q < CHIPS - 1
    has_up, has_down = strip > 0, strip < STRIPS - 1

    def device(dq, core, ds):
        return ((q + dq) * 2 + core, strip + ds)

    def side_ok(ds):
        return {0: None, -1: has_up, 1: has_down}[ds]

    def chip_ok(dq):
        return {0: None, -1: has_prev, 1: has_next}[dq]

    def by_core(x):
        if isinstance(x, tuple):
            return jnp.where(c == 0, x[0], x[1])
        return x

    barrier = pltpu.get_barrier_semaphore()
    last, mid = CHIPS - 1, CHIPS // 2

    def hello(semaphore, chip, core, row):
        pl.semaphore_signal(semaphore, inc=1, device_id=(chip * 2 + core, row), device_id_type=MESH)

    def hello_both(semaphore, chip):
        for core in range(2):
            hello(semaphore, chip, core, strip)

    pl.when(q == 0)(lambda: hello_both(barrier, mid))
    pl.when(q == mid - 1)(lambda: hello_both(barrier, last))

    def waits_apart(chip):
        return jnp.logical_and(chip % 8 >= 3, chip % 8 <= 3)

    when(has_prev, jnp.logical_not(waits_apart(q - 1)))(lambda: hello_both(barrier, q - 1))
    when(has_next)(lambda: hello_both(barrier, q + 1))
    when(has_up)(lambda: hello(barrier, q, c, strip - 1))
    when(has_down)(lambda: hello(barrier, q, c, strip + 1))
    hello(barrier, q, other, strip)

    own_copy = pltpu.make_async_copy(
        slc.at[:, :, :, pl.ds(pl.multiple_of(c * HALF, HALF), HALF)], tiles.at[1, pl.ds(2 * c, 2)], lsem
    )
    own_copy.start()
    second_copy = pltpu.make_async_copy(second_in, second, sem2.at[0])
    count_copy = pltpu.make_async_copy(count_in, count, sem2.at[1])
    second_copy.start()
    count_copy.start()

    def as_int(x):
        return jnp.where(x, 1, 0)

    apart = jnp.logical_and(has_next, waits_apart(q))
    greeted = 1 + 2 * (as_int(has_prev) + as_int(has_next) - as_int(apart)) + as_int(has_up) + as_int(has_down)
    pl.semaphore_wait(barrier, greeted + 2 * as_int(jnp.logical_or(q == mid, q == last)))
    when(has_prev, waits_apart(q - 1))(lambda: hello_both(ready, q - 1))
    pl.when(q == last)(lambda: hello_both(ready, mid - 1))

    swap = pltpu.make_async_remote_copy(
        src_ref=slc.at[:, :, :, pl.ds(pl.multiple_of(other * HALF, HALF), HALF)],
        dst_ref=tiles.at[1, pl.ds(2 * c, 2)],
        send_sem=xs,
        recv_sem=xr,
        device_id=device(0, other, 0),
        device_id_type=MESH,
    )

    PASSED = {-1: [(2, None), (3, 0), (3, 1)], 1: [(2, None)]}

    def tile_copy(dq, j, core, relay, part):
        send, recv = (us.at[j, core], ur) if dq < 0 else (vs.at[j, core], vr)
        if part == 1:
            send = us2 if dq < 0 else vs2
        chip = q + dq
        if relay:
            chip = 0 if dq < 0 else last
        if relay:
            recv = vr if dq < 0 else ur
        if part == 1:
            recv = {0: ur2, 1: vr2}[0 if recv is ur else 1]
        start_, width = (0, HALF) if part is None else (part * HALF // 2, HALF // 2)
        return pltpu.make_async_remote_copy(
            src_ref=slc.at[j, :, :, pl.ds(core * HALF + start_, width)],
            dst_ref=tiles.at[1 + dq if relay else 1 - dq, 2 * c + j, :, :, pl.ds(start_, width)],
            send_sem=send,
            recv_sem=recv.at[2 * c + j],
            device_id=(chip * 2 + core, strip),
            device_id_type=MESH,
        )

    def part_of(ref, part):
        if part is None:
            return ref
        return ref.at[:, :, pl.ds(part * HALF // 2, HALF // 2)]

    def forward_copy(n, at_first):
        which, part = PASSED[-1 if at_first else 1][n]
        step = which - 2
        a = by_core((NEXT if at_first else PREV)[2 + step])
        side = 2 if at_first else 0
        came, recv = (vr, ur) if at_first else (ur, vr)
        if part == 1:
            came, recv = (vr2, ur2) if at_first else (ur2, vr2)
        here = part_of(tiles.at[2 - side, a], part)
        copy = pltpu.make_async_remote_copy(
            src_ref=here,
            dst_ref=part_of(tiles.at[side, a], part),
            send_sem=fs.at[n],
            recv_sem=recv.at[a],
            device_id=((mid - 1 if at_first else mid) * 2 + c, strip),
            device_id_type=MESH,
        )
        return here, came.at[a], copy

    def pass_on(n):
        def one(at_first):
            here, came, copy = forward_copy(n, at_first)
            pltpu.make_async_copy(here, here, came).wait()
            copy.start()

        if n < len(PASSED[-1]):
            pl.when(q == 0)(lambda: one(True))
        if n < len(PASSED[1]):
            pl.when(q == last)(lambda: one(False))

    def passed_on(n):
        if n < len(PASSED[-1]):
            pl.when(q == 0)(lambda: forward_copy(n, True)[2].wait_send())
        if n < len(PASSED[1]):
            pl.when(q == last)(lambda: forward_copy(n, False)[2].wait_send())

    def tile_sends(act, times=(0, 1)):
        for here in range(2):

            @pl.when(c == here)
            def _():
                for n in range(4):
                    for dq in (-1, 1):
                        j = n // 2 if dq < 0 else 1 - n // 2
                        core = (here + n) % 2

                        far = q == (mid if dq < 0 else mid - 1)

                        def send_parts(relay):
                            for part in (0, 1) if n == 3 else (None,):
                                if relay is None or relay == ((n, part) in PASSED[dq]):
                                    act(tile_copy(dq, j, core, bool(relay), part))

                        for time in times:
                            if dq < 0:
                                if time == 0:
                                    when(has_prev, jnp.logical_not(far))(lambda: send_parts(None))
                                    when(far)(lambda: send_parts(False))
                                    when(far)(lambda: send_parts(True))
                            else:
                                waiting = apart if time == 1 else jnp.logical_not(apart)
                                when(has_next, waiting, jnp.logical_not(far))(lambda: send_parts(None))
                                when(far)(lambda: send_parts(time == 1))

    def start(copy):
        copy.start()

    def wait_send(copy):
        copy.wait_send()

    tile_sends(start, (0,))
    swap.start()

    first = lax.broadcasted_iota(jnp.int32, (CELLS, CELLS), 1) * LOOK_RG
    lane = lax.broadcasted_iota(jnp.int32, (CELLS, CELLS), 0)

    def fill(i, carry):
        delta = lane + i * CELLS - first
        inside = jnp.logical_and(delta >= 0, delta < LOOK_RG)
        table[pl.ds(pl.multiple_of(i * CELLS, CELLS), CELLS), :] = jnp.where(inside, 1.0, 0.0).astype(BF16)
        return carry

    lax.fori_loop(0, WIDTH // CELLS, fill, 0)

    @pl.when(jnp.logical_or(apart, q == mid - 1))
    def _():
        pl.semaphore_wait(ready, 2)
        tile_sends(start, (1,))

    row = lax.broadcasted_iota(jnp.int32, (ROWS, ROWS), 0)
    col = lax.broadcasted_iota(jnp.int32, (ROWS, ROWS), 1)
    order = jnp.where(col == LOOK_AZ * (row % LOOKS) + row // LOOKS, 1.0, 0.0).astype(BF16)
    sub = lax.broadcasted_iota(jnp.int32, (LOOKS, CELLS), 0)
    lane8 = lax.broadcasted_iota(jnp.int32, (LOOKS, CELLS), 1)
    left = lane8 < CELLS // 2

    @pl.when(jnp.logical_not(has_up))
    def _():
        edge[0] = jnp.zeros(edge.shape[1:], F32)

    @pl.when(jnp.logical_not(has_down))
    def _():
        edge[1] = jnp.zeros(edge.shape[1:], F32)

    def get_tile(rel, a, part):
        @when(chip_ok(rel))
        def _():
            whole, second_half = (ur, ur2) if rel > 0 else (vr, vr2)
            ref = part_of(tiles.at[1 + rel, a], part)
            pltpu.make_async_copy(ref, ref, (second_half if part == 1 else whole).at[a]).wait()
            reorder(rel, a, part)

    def reorder(rel, a, part):
        at = slice(None) if part is None else pl.ds(part * HALF // 2, HALF // 2)
        for i in range(2):
            looks[1 + rel, a, i, :, at] = jnp.dot(order, tiles[1 + rel, a, i, :, at], preferred_element_type=F32)

    def rims(x):
        d = jnp.where(sub < 3, pltpu.roll(x, 3, 0), 0.0)
        d = d + pltpu.roll(d, LOOKS - 1, 0) + pltpu.roll(d, LOOKS - 2, 0)
        u = jnp.where(jnp.logical_and(sub >= 1, sub < 4), pltpu.roll(x, 1, 0), 0.0)
        u = u + pltpu.roll(u, 1, 0) + pltpu.roll(u, 2, 0)
        return d[0:4], u[0:4]

    def planes_of(stage, own, far):
        planes = list(STAGES[stage]) if own else []
        if far:
            for (pair0, _), (pair1, _) in BACK[stage]:
                planes.append(pair((-1, (pair0[0], pair1[0])), (1, (pair0[1], pair1[1]))))
        return [(kind, (u[0], by_core(u[1])), (v[0], by_core(v[1]))) for kind, u, v in planes]

    def looked(planes, at0, part):
        n = len(planes)
        m = n + n % 2

        def lanes(t, carry):
            at = pl.ds(pl.multiple_of(t * CELLS, CELLS), CELLS)
            at2 = pl.ds(pl.multiple_of(t * CELLS + HALF, CELLS), CELLS)

            def total(x):
                return jnp.sum(x.reshape(LOOK_AZ, LOOKS, CELLS), axis=0)

            for i, (kind, u, v) in enumerate(planes):
                u_r, u_i = looks[1 + u[0], u[1], 0, :, at], looks[1 + u[0], u[1], 1, :, at]
                v_r, v_i = looks[1 + v[0], v[1], 0, :, at], looks[1 + v[0], v[1], 1, :, at]
                if kind == "pair":
                    x, y = u_r * v_r + u_i * v_i, u_i * v_r - u_r * v_i
                else:
                    x, y = u_r * u_r + u_i * u_i, v_r * v_r + v_i * v_i
                sums[at0 + i, :, at] = total(x)
                sums[at0 + i, :, at2] = total(y)
            return carry

        steps = HALF // CELLS
        spans = [(0, WIDTH)]
        first_, end = 0, steps
        if part is not None:
            spans = [(part * HALF // 2, HALF // 2), (HALF + part * HALF // 2, HALF // 2)]
            first_, end = part * steps // 2, (part + 1) * steps // 2
        lax.fori_loop(first_, end, lanes, 0)
        if m > n:
            sums[at0 + n] = jnp.zeros((LOOKS, WIDTH), F32)
        out = None
        for at, width in spans:
            x = sums[at0 : at0 + m, :, at : at + width].reshape(m * LOOKS, width)
            hi = x.astype(BF16)
            lo = (x - hi.astype(F32)).astype(BF16)
            t = table[at : at + width, :]
            y = jnp.dot(hi, t, preferred_element_type=F32) + jnp.dot(lo, t, preferred_element_type=F32)
            out = y if out is None else out + y
        return out

    def as_planes(out):
        return (out * PLANE_SCALE).reshape(out.shape[0] // LOOKS, LOOKS, CELLS)

    def put_back(places, out):
        for i, place in places:
            place = by_core(place)
            back[place] = out[i]
            back_rim[0, place], back_rim[1, place] = rims(out[i])

    def put_own(stage, out):
        for i in range(len(STAGES[stage])):
            res[c, STARTS[stage] + i] = out[i]
            rim[0, STARTS[stage] + i], rim[1, STARTS[stage] + i] = rims(out[i])
        if stage in BACK_POWER:
            put_back([(2, both) for both in zip(*BACK_POWER[stage], strict=True)], out)

    def put_far(stage, out):
        put_back([(i, (p0, p1)) for i, ((_, p0), (_, p1)) in enumerate(BACK[stage])], out)

    def compute(stage):
        out = as_planes(looked(planes_of(stage, True, True), 0, None))
        put_own(stage, out)
        put_far(stage, out[len(STAGES[stage]) :])

    def span_of(stage, core):
        if stage == 0:
            return pl.ds(0, 8)
        return pl.ds(STARTS[stage] + 2 * core, NEEDS[stage][0][1])

    def core_send(stage):
        return pltpu.make_async_remote_copy(
            src_ref=res.at[c, span_of(stage, other)],
            dst_ref=res.at[c, span_of(stage, other)],
            send_sem=ps.at[stage],
            recv_sem=pr.at[stage],
            device_id=device(0, other, 0),
            device_id_type=MESH,
        )

    def rim_send(stage, core, ds):
        first_, size = NEEDS[stage][core]
        side = (1 - ds) // 2
        span = pl.ds(STARTS[stage] + first_, size)
        return pltpu.make_async_remote_copy(
            src_ref=rim.at[side, span],
            dst_ref=edge.at[side, c, span],
            send_sem=hs.at[stage, core, side],
            recv_sem=hr.at[stage],
            device_id=device(0, core, ds),
            device_id_type=MESH,
        )

    def back_send(m, ds):
        _, _, core, first_, size = BACK_SENDS[m]
        span, there = pl.ds(first_, size), pl.ds(N_OWN + first_, size)
        if ds == 0:
            src, dst = back.at[span], res.at[c, there]
        else:
            side = (1 - ds) // 2
            src, dst = back_rim.at[side, span], edge.at[side, c, there]
        return pltpu.make_async_remote_copy(
            src_ref=src,
            dst_ref=dst,
            send_sem=bs.at[m, 1 + ds],
            recv_sem=br.at[m, 0 if ds == 0 else 1],
            device_id=device(-1, core, ds),
            device_id_type=MESH,
        )

    def back_sends(stage, act):
        for here in range(2):
            specs = [m for m, spec in enumerate(BACK_SENDS) if spec[0] == stage and spec[1] == here]
            if specs:

                @when(c == here, has_prev)
                def _():
                    for ds in (-1, 1, 0):

                        @when(side_ok(ds))
                        def _():
                            for m in specs:
                                act(back_send(m, ds))

    def own_sends(stage, act):
        for ds in (-1, 1):

            @when(side_ok(ds))
            def _():
                for core in range(2):
                    act(rim_send(stage, core, ds))

        act(core_send(stage))

    def all_sends(stage, act):
        back_sends(stage, act)
        own_sends(stage, act)

    def wait_for(ref, sem):
        pltpu.make_async_copy(ref, ref, sem).wait()

    def edge_wait(h, span, sem):
        here = edge if h is None else edge.at[:, pl.ds(h, 1)]
        when(has_up, has_down)(lambda: wait_for(here.at[:, :, span], sem))
        when(jnp.logical_not(has_up))(lambda: wait_for(here.at[1, :, span], sem))
        when(jnp.logical_not(has_down))(lambda: wait_for(here.at[0, :, span], sem))

    def own_arrivals(stage):
        wait_for(res.at[other, span_of(stage, c)], pr.at[stage])
        if stage == 0:
            for core in range(2):
                first_, size = NEEDS[0][core]
                pl.when(c == core)(lambda: edge_wait(None, pl.ds(first_, size), hr.at[0]))
        else:
            edge_wait(None, span_of(stage, c), hr.at[stage])

    def back_arrivals(stage):
        for core in range(2):

            @when(has_next, c == core)
            def _():
                for m, (after, h, to, first_, size) in enumerate(BACK_SENDS):
                    if after == stage and to == core:
                        span = pl.ds(N_OWN + first_, size)
                        wait_for(res.at[h, span], br.at[m, 0])
                        edge_wait(h, span, br.at[m, 1])

    def low(p0, p1):
        return jnp.where(left, p0, pltpu.roll(p1, CELLS // 2, 1))

    def high(p0, p1):
        return jnp.where(left, pltpu.roll(p0, CELLS // 2, 1), p1)

    def rows_box(h, plane):
        x = res[h, plane]
        total = x + jnp.concatenate([edge[0, h, plane], edge[1, h, plane]], axis=0)
        for k in range(1, 4):
            total = total + jnp.where(sub >= k, pltpu.roll(x, k, 0), 0.0)
            total = total + jnp.where(sub < LOOKS - k, pltpu.roll(x, LOOKS - k, 0), 0.0)
        return total

    def cells_box(x):
        total = x
        for k in range(1, 4):
            total = total + jnp.where(lane8 >= k, pltpu.roll(x, k, 1), 0.0)
            total = total + jnp.where(lane8 < CELLS - k, pltpu.roll(x, CELLS - k, 1), 0.0)
        return total

    def ref_boxes():
        for j in range(2):
            r0, r1 = rows_box(0, 5 + j), rows_box(1, 5 + j)
            box_ref[j] = cells_box(jnp.where(c == 0, low(r0, r1), high(r0, r1)))

    def coherences(step):
        for core in range(2):

            @pl.when(c == core)
            def _():
                for j, off, place, sec, half in finals(core, step):
                    p0, p1 = res[0, place[0]], res[1, place[1]]
                    every_ifg[j, off - 1, 0] = low(p0, p1)
                    every_ifg[j, off - 1, 1] = high(p0, p1)
                    b0, b1 = rows_box(0, place[0]), rows_box(1, place[1])
                    s0, s1 = rows_box(0, sec[0]), rows_box(1, sec[1])
                    box_r, box_i = cells_box(low(b0, b1)), cells_box(high(b0, b1))
                    box_s = cells_box(high(s0, s1) if half else low(s0, s1))
                    top = jnp.sqrt(box_r * box_r + box_i * box_i)
                    every_coh[j, off - 1] = top / jnp.sqrt(box_ref[j] * box_s)

    own_copy.wait()
    second_copy.wait()
    count_copy.wait()
    chosen = []
    for j in range(2):
        for slot in range(SLOTS):
            off = jnp.clip(second[j, slot] - (4 * q + 2 * c + j), 1, OFFS)
            chosen.append((j, slot, off - 1, slot < count[j]))
    swap.wait_recv()
    for a in range(4):
        reorder(0, a, None)
    compute(0)
    all_sends(0, start)
    swap.wait_send()
    for stage in range(1, 5):
        b, a = by_core(NEXT[stage - 1]), by_core(PREV[stage - 1])
        if stage < 4:
            get_tile(1, b, None)
            get_tile(-1, a, None)
            compute(stage)
            all_sends(stage, start)
        else:
            own, far = planes_of(4, True, False), planes_of(4, False, True)
            get_tile(1, b, 0)
            own_out = looked(own, 0, 0)
            get_tile(-1, a, 0)
            far_out = looked(far, 6, 0)
            get_tile(1, b, 1)
            put_own(4, as_planes(own_out + looked(own, 0, 1)))
            own_sends(4, start)
            get_tile(-1, a, 1)
            put_far(4, as_planes(far_out + looked(far, 6, 1)))
            back_sends(4, start)
        if stage == 1:
            pass_on(0)
        if stage == 2:
            pass_on(1)
            pass_on(2)
        all_sends(stage - 1, wait_send)
        own_arrivals(stage - 1)
        if stage == 1:
            ref_boxes()
            coherences(0)
        if stage == 3:
            coherences(1)
    tile_sends(wait_send)
    for n in range(3):
        passed_on(n)
    own_arrivals(4)
    coherences(2)
    back_arrivals(3)
    coherences(3)
    back_arrivals(4)
    coherences(4)

    zero = jnp.zeros((LOOKS, CELLS), F32)
    for j, slot, off, used in chosen:
        for part in range(2):
            ifg[j, slot, part] = jnp.where(used, every_ifg[j, off, part], zero)
        coh[j, slot] = jnp.where(used, every_coh[j, off], zero)

    all_sends(4, wait_send)


def store_kernel(ifg, coh, ifg_out, coh_out, sems):
    copies = [
        pltpu.make_async_copy(ifg, ifg_out, sems.at[0]),
        pltpu.make_async_copy(coh, coh_out, sems.at[1]),
    ]
    for copy in copies:
        copy.start()
    for copy in copies:
        copy.wait()


def shards(slc, pair_second, pair_count):
    dma = pltpu.SemaphoreType.DMA
    hbm = pl.BlockSpec(memory_space=pltpu.HBM)
    vmem = pl.BlockSpec(memory_space=pltpu.VMEM)
    ifg_shape = (2, SLOTS, 2, LOOKS, CELLS)
    coh_shape = (2, SLOTS, LOOKS, CELLS)
    operands = [pltpu.with_memory_space_constraint(x, pltpu.HBM) for x in (slc, pair_second, pair_count)]
    ifg, coh = pl.pallas_call(
        planes_kernel,
        out_shape=(pltpu.VMEM(ifg_shape, F32), pltpu.VMEM(coh_shape, F32)),
        in_specs=[hbm, hbm, hbm],
        out_specs=(vmem, vmem),
        scratch_shapes=[
            pltpu.VMEM((2, N_PLANES, LOOKS, CELLS), F32),
            pltpu.VMEM((2, 2, N_PLANES, 4, CELLS), F32),
            pltpu.VMEM((3, 4, 2, ROWS, HALF), BF16),
            pltpu.VMEM((3, 4, 2, ROWS, HALF), F32),
            pltpu.VMEM((10, LOOKS, WIDTH), F32),
            pltpu.VMEM((WIDTH, CELLS), BF16),
            pltpu.VMEM((N_BACK, LOOKS, CELLS), F32),
            pltpu.VMEM((2, N_OWN, 4, CELLS), F32),
            pltpu.VMEM((2, N_BACK, 4, CELLS), F32),
            pltpu.SMEM((2, SLOTS), jnp.int32),
            pltpu.SMEM((2,), jnp.int32),
            pltpu.VMEM((2, OFFS, 2, LOOKS, CELLS), F32),
            pltpu.VMEM((2, OFFS, LOOKS, CELLS), F32),
            pltpu.VMEM((2, LOOKS, CELLS), F32),
            pltpu.SemaphoreType.REGULAR,
            dma,
            dma((2,)),
            dma,
            dma,
            dma((2, 2)),
            dma((4,)),
            dma((2, 2)),
            dma((4,)),
            dma,
            dma((4,)),
            dma,
            dma((4,)),
            dma((3,)),
            dma((5,)),
            dma((5,)),
            dma((5, 2, 2)),
            dma((5,)),
            dma((8, 3)),
            dma((8, 2)),
        ],
        compiler_params=pltpu.CompilerParams(
            collective_id=0, has_side_effects=True, vmem_limit_bytes=40 * 2**20
        ),
    )(*operands)
    return pl.pallas_call(
        store_kernel,
        out_shape=(jax.ShapeDtypeStruct(ifg_shape, F32), jax.ShapeDtypeStruct(coh_shape, F32)),
        in_specs=[vmem, vmem],
        out_specs=(pl.BlockSpec(memory_space=pl.ANY), pl.BlockSpec(memory_space=pl.ANY)),
        scratch_shapes=[dma((2,))],
        compiler_params=pltpu.CompilerParams(vmem_limit_bytes=16 * 2**20),
    )(ifg, coh)


def solution(mesh):
    in_specs = (P("date", None, "strip", None), P("date", None), P("date"))
    out_specs = (P("date", None, None, "strip", None), P("date", None, "strip", None))
    return jax.shard_map(shards, mesh=mesh, in_specs=in_specs, out_specs=out_specs, check_vma=False)
```

```python
import jax
import jax.numpy as jnp
from jax import lax
from jax.experimental import pallas as pl
from jax.experimental.pallas import tpu as pltpu
from jax.sharding import PartitionSpec as P

MESH = pl.DeviceIdType.MESH
F32 = jnp.float32
BF16 = jnp.bfloat16

LOOK_AZ = 5
LOOK_RG = 20
SLOTS = 6
OFFS = 8
CHIPS = 16
STRIPS = 8
ROWS = 40
WIDTH = 2560
HALF = WIDTH // 2
LOOKS = ROWS // LOOK_AZ
CELLS = 128
PLANE_SCALE = 1.0 / (LOOK_AZ * LOOK_RG)


def pair(a, b):
    return ("pair", a, b)


def power(a, b):
    return ("power", a, b)


def onto(b, *middle):
    return [pair((0, 0), (1, b)), pair((0, 1), (1, b)), *middle, pair((0, 2), (1, b)), pair((0, 3), (1, b))]


NEXT = [(0, 2), (2, 0), (1, 3), (3, 1)]
PREV = [(1, 3), (3, 1), (0, 2), (2, 0)]
SAME = [(0, 1), (0, 2), (0, 3), (1, 2), (1, 3)]
STAGES = [
    [pair((0, a), (0, b)) for a, b in SAME] + [power((0, 0), (0, 2)), power((0, 1), (0, 3)), pair((0, 2), (0, 3))],
    onto(NEXT[0]),
    onto(NEXT[1], power((1, 0), (1, 2))),
    onto(NEXT[2]),
    onto(NEXT[3], power((1, 1), (1, 3))),
]
STARTS = [0, 8, 12, 17, 21]
NEEDS = [[(0, 7), (5, 3)], [(0, 2), (2, 2)], [(0, 3), (2, 3)], [(0, 2), (2, 2)], [(0, 3), (2, 3)]]
N_OWN = 26
IA, IB = 14, 23
BACK = [
    [],
    [(((1, 0), 0), ((3, 2), 2))],
    [(((3, 0), 4), ((3, 0), 3)), (((3, 2), 5), ((1, 0), 0))],
    [(((0, 0), 1), ((3, 3), 4)), (((1, 1), 2), ((2, 0), 5)), (((3, 1), 6), ((2, 2), 6))],
    [(((2, 0), 10), ((3, 1), 12)), (((2, 2), 11), ((2, 1), 13)), (((2, 1), 12), ((1, 1), 9)), (((3, 3), 13), ((0, 0), 10))],
]
BACK_POWER = {2: [(3, 7), (1, 7)], 4: [(8, 9), (8, 11)]}
N_BACK = 14
BACK_SENDS = [
    (3, 0, 0, 0, 4),
    (3, 0, 1, 4, 4),
    (3, 1, 0, 0, 2),
    (3, 1, 1, 2, 6),
    (4, 0, 0, 8, 1),
    (4, 0, 1, 9, 5),
    (4, 1, 0, 8, 3),
    (4, 1, 1, 11, 3),
]
FAR = [{}, {}]
for stage_ in BACK:
    for both_ in stage_:
        for core_ in range(2):
            FAR[core_][both_[core_][0]] = both_[core_][1]
N_PLANES = N_OWN + N_BACK


def arrival(b, core):
    return 1 + [x[core] for x in NEXT].index(b)


def finals(core, when_):
    found = []
    for j in range(2):
        a = 2 * core + j
        for off in range(1, OFFS + 1):
            chip, e = divmod(a + off, 4)
            odd, half = e % 2, e // 2
            if chip == 0:
                step, place = 0, [(SAME + [None, None, (2, 3)]).index((a, e))] * 2
                sec = [6 if odd else 5] * 2
            elif chip == 1:
                step, place = 2 if odd else 1, []
                for h in range(2):
                    t = arrival(e, h)
                    place.append(STARTS[t] + a + (1 if t % 2 == 0 and a >= 2 else 0))
                sec = [IB if odd else IA] * 2
            else:
                place = [N_OWN + FAR[h][(a, e)] for h in range(2)]
                late = any(spec[0] == 4 and spec[1] == h and spec[3] <= FAR[h][(a, e)] < spec[3] + spec[4] for spec in BACK_SENDS for h in range(2))
                step = 4 if late or odd else 3
                sec = [N_OWN + BACK_POWER[4 if odd else 2][h][core] for h in range(2)]
            if step == when_:
                found.append((j, off, place, sec, half))
    return found


def when(*conditions):
    conditions = [x for x in conditions if x is not None]
    if not conditions:
        return lambda f: f()
    total = conditions[0]
    for x in conditions[1:]:
        total = jnp.logical_and(total, x)
    return pl.when(total)


def planes_kernel(
    slc, second_in, count_in, ifg, coh, res, edge, tiles, looks, sums, table, back, rim, back_rim, second, count, every_ifg, every_coh, box_ref,
    ready, lsem, sem2, xs, xr, us, ur, vs, vr, us2, ur2, vs2, vr2, fs, ps, pr, hs, hr, bs, br,
):
    date = lax.axis_index("date")
    strip = lax.axis_index("strip")
    q = date // 2
    c = date % 2
    other = 1 - c
    has_prev, has_next = q > 0, q < CHIPS - 1
    has_up, has_down = strip > 0, strip < STRIPS - 1

    def device(dq, core, ds):
        return ((q + dq) * 2 + core, strip + ds)

    def side_ok(ds):
        return {0: None, -1: has_up, 1: has_down}[ds]

    def chip_ok(dq):
        return {0: None, -1: has_prev, 1: has_next}[dq]

    def by_core(x):
        if isinstance(x, tuple):
            return jnp.where(c == 0, x[0], x[1])
        return x

    barrier = pltpu.get_barrier_semaphore()
    last, mid = CHIPS - 1, CHIPS // 2

    def hello(semaphore, chip, core, row):
        pl.semaphore_signal(semaphore, inc=1, device_id=(chip * 2 + core, row), device_id_type=MESH)

    def hello_both(semaphore, chip):
        for core in range(2):
            hello(semaphore, chip, core, strip)

    pl.when(q == 0)(lambda: hello_both(barrier, mid))
    pl.when(q == mid - 1)(lambda: hello_both(barrier, last))

    def waits_apart(chip):
        return jnp.logical_and(chip % 8 >= 3, chip % 8 <= 3)

    when(has_prev, jnp.logical_not(waits_apart(q - 1)))(lambda: hello_both(barrier, q - 1))
    when(has_next, q != mid - 1)(lambda: hello_both(barrier, q + 1))
    when(has_up)(lambda: hello(barrier, q, c, strip - 1))
    when(has_down)(lambda: hello(barrier, q, c, strip + 1))
    hello(barrier, q, other, strip)

    own_copy = pltpu.make_async_copy(
        slc.at[:, :, :, pl.ds(pl.multiple_of(c * HALF, HALF), HALF)], tiles.at[1, pl.ds(2 * c, 2)], lsem
    )
    own_copy.start()
    second_copy = pltpu.make_async_copy(second_in, second, sem2.at[0])
    count_copy = pltpu.make_async_copy(count_in, count, sem2.at[1])
    second_copy.start()
    count_copy.start()

    def as_int(x):
        return jnp.where(x, 1, 0)

    apart = jnp.logical_and(has_next, waits_apart(q))
    greeted = 1 + 2 * (as_int(has_prev) + as_int(has_next) - as_int(apart) - as_int(q == mid)) + as_int(has_up) + as_int(has_down)
    pl.semaphore_wait(barrier, greeted + 2 * as_int(jnp.logical_or(q == mid, q == last)))
    when(has_prev, waits_apart(q - 1))(lambda: hello_both(ready, q - 1))
    pl.when(q == last)(lambda: hello_both(ready, mid - 1))
    pl.when(q == mid - 1)(lambda: hello_both(ready, mid))

    swap = pltpu.make_async_remote_copy(
        src_ref=slc.at[:, :, :, pl.ds(pl.multiple_of(other * HALF, HALF), HALF)],
        dst_ref=tiles.at[1, pl.ds(2 * c, 2)],
        send_sem=xs,
        recv_sem=xr,
        device_id=device(0, other, 0),
        device_id_type=MESH,
    )

    PASSED = {-1: [(2, None), (3, 1)], 1: [(2, None)]}

    def tile_copy(dq, j, core, relay, part):
        send, recv = (us.at[j, core], ur) if dq < 0 else (vs.at[j, core], vr)
        if part == 1:
            send = us2 if dq < 0 else vs2
        chip = q + dq
        if relay:
            chip = 0 if dq < 0 else last
        if relay:
            recv = vr if dq < 0 else ur
        if part == 1:
            recv = {0: ur2, 1: vr2}[0 if recv is ur else 1]
        start_, width = (0, HALF) if part is None else (part * HALF // 2, HALF // 2)
        return pltpu.make_async_remote_copy(
            src_ref=slc.at[j, :, :, pl.ds(core * HALF + start_, width)],
            dst_ref=tiles.at[1 + dq if relay else 1 - dq, 2 * c + j, :, :, pl.ds(start_, width)],
            send_sem=send,
            recv_sem=recv.at[2 * c + j],
            device_id=(chip * 2 + core, strip),
            device_id_type=MESH,
        )

    def part_of(ref, part):
        if part is None:
            return ref
        return ref.at[:, :, pl.ds(part * HALF // 2, HALF // 2)]

    def forward_copy(n, at_first):
        which, part = PASSED[-1 if at_first else 1][n]
        step = which - 2
        a = by_core((NEXT if at_first else PREV)[2 + step])
        side = 2 if at_first else 0
        came, recv = (vr, ur) if at_first else (ur, vr)
        if part == 1:
            came, recv = (vr2, ur2) if at_first else (ur2, vr2)
        here = part_of(tiles.at[2 - side, a], part)
        copy = pltpu.make_async_remote_copy(
            src_ref=here,
            dst_ref=part_of(tiles.at[side, a], part),
            send_sem=fs.at[n],
            recv_sem=recv.at[a],
            device_id=((mid - 1 if at_first else mid) * 2 + c, strip),
            device_id_type=MESH,
        )
        return here, came.at[a], copy

    def pass_on(n):
        def one(at_first):
            here, came, copy = forward_copy(n, at_first)
            pltpu.make_async_copy(here, here, came).wait()
            copy.start()

        if n < len(PASSED[-1]):
            pl.when(q == 0)(lambda: one(True))
        if n < len(PASSED[1]):
            pl.when(q == last)(lambda: one(False))

    def passed_on(n):
        if n < len(PASSED[-1]):
            pl.when(q == 0)(lambda: forward_copy(n, True)[2].wait_send())
        if n < len(PASSED[1]):
            pl.when(q == last)(lambda: forward_copy(n, False)[2].wait_send())

    def tile_sends(act, times=(0, 1)):
        for here in range(2):

            @pl.when(c == here)
            def _():
                for n in range(4):
                    for dq in (-1, 1):
                        j = n // 2 if dq < 0 else 1 - n // 2
                        core = (here + n) % 2

                        far = q == (mid if dq < 0 else mid - 1)

                        def send_parts(relay):
                            for part in (0, 1) if n == 3 else (None,):
                                if relay is None or relay == ((n, part) in PASSED[dq]):
                                    act(tile_copy(dq, j, core, bool(relay), part))

                        for time in times:
                            if dq < 0:
                                if time == 0:
                                    when(has_prev, jnp.logical_not(far))(lambda: send_parts(None))
                                else:
                                    when(far)(lambda: send_parts(False))
                                    when(far)(lambda: send_parts(True))
                            else:
                                waiting = apart if time == 1 else jnp.logical_not(apart)
                                when(has_next, waiting, jnp.logical_not(far))(lambda: send_parts(None))
                                when(far)(lambda: send_parts(time == 1))

    def start(copy):
        copy.start()

    def wait_send(copy):
        copy.wait_send()

    tile_sends(start, (0,))
    swap.start()

    first = lax.broadcasted_iota(jnp.int32, (CELLS, CELLS), 1) * LOOK_RG
    lane = lax.broadcasted_iota(jnp.int32, (CELLS, CELLS), 0)

    def fill(i, carry):
        delta = lane + i * CELLS - first
        inside = jnp.logical_and(delta >= 0, delta < LOOK_RG)
        table[pl.ds(pl.multiple_of(i * CELLS, CELLS), CELLS), :] = jnp.where(inside, 1.0, 0.0).astype(BF16)
        return carry

    lax.fori_loop(0, WIDTH // CELLS, fill, 0)

    @pl.when(jnp.logical_or(apart, jnp.logical_or(q == mid - 1, q == mid)))
    def _():
        pl.semaphore_wait(ready, 2)
        tile_sends(start, (1,))

    row = lax.broadcasted_iota(jnp.int32, (ROWS, ROWS), 0)
    col = lax.broadcasted_iota(jnp.int32, (ROWS, ROWS), 1)
    order = jnp.where(col == LOOK_AZ * (row % LOOKS) + row // LOOKS, 1.0, 0.0).astype(BF16)
    sub = lax.broadcasted_iota(jnp.int32, (LOOKS, CELLS), 0)
    lane8 = lax.broadcasted_iota(jnp.int32, (LOOKS, CELLS), 1)
    left = lane8 < CELLS // 2

    @pl.when(jnp.logical_not(has_up))
    def _():
        edge[0] = jnp.zeros(edge.shape[1:], F32)

    @pl.when(jnp.logical_not(has_down))
    def _():
        edge[1] = jnp.zeros(edge.shape[1:], F32)

    def get_tile(rel, a, part):
        @when(chip_ok(rel))
        def _():
            whole, second_half = (ur, ur2) if rel > 0 else (vr, vr2)
            ref = part_of(tiles.at[1 + rel, a], part)
            pltpu.make_async_copy(ref, ref, (second_half if part == 1 else whole).at[a]).wait()
            reorder(rel, a, part)

    def reorder(rel, a, part):
        at = slice(None) if part is None else pl.ds(part * HALF // 2, HALF // 2)
        for i in range(2):
            looks[1 + rel, a, i, :, at] = jnp.dot(order, tiles[1 + rel, a, i, :, at], preferred_element_type=F32)

    def rims(x):
        d = jnp.where(sub < 3, pltpu.roll(x, 3, 0), 0.0)
        d = d + pltpu.roll(d, LOOKS - 1, 0) + pltpu.roll(d, LOOKS - 2, 0)
        u = jnp.where(jnp.logical_and(sub >= 1, sub < 4), pltpu.roll(x, 1, 0), 0.0)
        u = u + pltpu.roll(u, 1, 0) + pltpu.roll(u, 2, 0)
        return d[0:4], u[0:4]

    def planes_of(stage, own, far):
        planes = list(STAGES[stage]) if own else []
        if far:
            for (pair0, _), (pair1, _) in BACK[stage]:
                planes.append(pair((-1, (pair0[0], pair1[0])), (1, (pair0[1], pair1[1]))))
        return [(kind, (u[0], by_core(u[1])), (v[0], by_core(v[1]))) for kind, u, v in planes]

    def looked(planes, at0, part):
        n = len(planes)
        m = n + n % 2

        def lanes(t, carry):
            at = pl.ds(pl.multiple_of(t * CELLS, CELLS), CELLS)
            at2 = pl.ds(pl.multiple_of(t * CELLS + HALF, CELLS), CELLS)

            def total(x):
                return jnp.sum(x.reshape(LOOK_AZ, LOOKS, CELLS), axis=0)

            for i, (kind, u, v) in enumerate(planes):
                u_r, u_i = looks[1 + u[0], u[1], 0, :, at], looks[1 + u[0], u[1], 1, :, at]
                v_r, v_i = looks[1 + v[0], v[1], 0, :, at], looks[1 + v[0], v[1], 1, :, at]
                if kind == "pair":
                    x, y = u_r * v_r + u_i * v_i, u_i * v_r - u_r * v_i
                else:
                    x, y = u_r * u_r + u_i * u_i, v_r * v_r + v_i * v_i
                sums[at0 + i, :, at] = total(x)
                sums[at0 + i, :, at2] = total(y)
            return carry

        steps = HALF // CELLS
        spans = [(0, WIDTH)]
        first_, end = 0, steps
        if part is not None:
            spans = [(part * HALF // 2, HALF // 2), (HALF + part * HALF // 2, HALF // 2)]
            first_, end = part * steps // 2, (part + 1) * steps // 2
        lax.fori_loop(first_, end, lanes, 0)
        if m > n:
            sums[at0 + n] = jnp.zeros((LOOKS, WIDTH), F32)
        out = None
        for at, width in spans:
            x = sums[at0 : at0 + m, :, at : at + width].reshape(m * LOOKS, width)
            hi = x.astype(BF16)
            lo = (x - hi.astype(F32)).astype(BF16)
            t = table[at : at + width, :]
            y = jnp.dot(hi, t, preferred_element_type=F32) + jnp.dot(lo, t, preferred_element_type=F32)
            out = y if out is None else out + y
        return out

    def as_planes(out):
        return (out * PLANE_SCALE).reshape(out.shape[0] // LOOKS, LOOKS, CELLS)

    def put_back(places, out):
        for i, place in places:
            place = by_core(place)
            back[place] = out[i]
            back_rim[0, place], back_rim[1, place] = rims(out[i])

    def put_own(stage, out):
        for i in range(len(STAGES[stage])):
            res[c, STARTS[stage] + i] = out[i]
            rim[0, STARTS[stage] + i], rim[1, STARTS[stage] + i] = rims(out[i])
        if stage in BACK_POWER:
            put_back([(2, both) for both in zip(*BACK_POWER[stage], strict=True)], out)

    def put_far(stage, out):
        put_back([(i, (p0, p1)) for i, ((_, p0), (_, p1)) in enumerate(BACK[stage])], out)

    def compute(stage):
        out = as_planes(looked(planes_of(stage, True, True), 0, None))
        put_own(stage, out)
        put_far(stage, out[len(STAGES[stage]) :])

    def span_of(stage, core):
        if stage == 0:
            return pl.ds(0, 8)
        return pl.ds(STARTS[stage] + 2 * core, NEEDS[stage][0][1])

    def core_send(stage):
        return pltpu.make_async_remote_copy(
            src_ref=res.at[c, span_of(stage, other)],
            dst_ref=res.at[c, span_of(stage, other)],
            send_sem=ps.at[stage],
            recv_sem=pr.at[stage],
            device_id=device(0, other, 0),
            device_id_type=MESH,
        )

    def rim_send(stage, core, ds):
        first_, size = NEEDS[stage][core]
        side = (1 - ds) // 2
        span = pl.ds(STARTS[stage] + first_, size)
        return pltpu.make_async_remote_copy(
            src_ref=rim.at[side, span],
            dst_ref=edge.at[side, c, span],
            send_sem=hs.at[stage, core, side],
            recv_sem=hr.at[stage],
            device_id=device(0, core, ds),
            device_id_type=MESH,
        )

    def back_send(m, ds):
        _, _, core, first_, size = BACK_SENDS[m]
        span, there = pl.ds(first_, size), pl.ds(N_OWN + first_, size)
        if ds == 0:
            src, dst = back.at[span], res.at[c, there]
        else:
            side = (1 - ds) // 2
            src, dst = back_rim.at[side, span], edge.at[side, c, there]
        return pltpu.make_async_remote_copy(
            src_ref=src,
            dst_ref=dst,
            send_sem=bs.at[m, 1 + ds],
            recv_sem=br.at[m, 0 if ds == 0 else 1],
            device_id=device(-1, core, ds),
            device_id_type=MESH,
        )

    def back_sends(stage, act):
        for here in range(2):
            specs = [m for m, spec in enumerate(BACK_SENDS) if spec[0] == stage and spec[1] == here]
            if specs:

                @when(c == here, has_prev)
                def _():
                    for ds in (-1, 1, 0):

                        @when(side_ok(ds))
                        def _():
                            for m in specs:
                                act(back_send(m, ds))

    def own_sends(stage, act):
        for ds in (-1, 1):

            @when(side_ok(ds))
            def _():
                for core in range(2):
                    act(rim_send(stage, core, ds))

        act(core_send(stage))

    def all_sends(stage, act):
        back_sends(stage, act)
        own_sends(stage, act)

    def wait_for(ref, sem):
        pltpu.make_async_copy(ref, ref, sem).wait()

    def edge_wait(h, span, sem):
        here = edge if h is None else edge.at[:, pl.ds(h, 1)]
        when(has_up, has_down)(lambda: wait_for(here.at[:, :, span], sem))
        when(jnp.logical_not(has_up))(lambda: wait_for(here.at[1, :, span], sem))
        when(jnp.logical_not(has_down))(lambda: wait_for(here.at[0, :, span], sem))

    def own_arrivals(stage):
        wait_for(res.at[other, span_of(stage, c)], pr.at[stage])
        if stage == 0:
            for core in range(2):
                first_, size = NEEDS[0][core]
                pl.when(c == core)(lambda: edge_wait(None, pl.ds(first_, size), hr.at[0]))
        else:
            edge_wait(None, span_of(stage, c), hr.at[stage])

    def back_arrivals(stage):
        for core in range(2):

            @when(has_next, c == core)
            def _():
                for m, (after, h, to, first_, size) in enumerate(BACK_SENDS):
                    if after == stage and to == core:
                        span = pl.ds(N_OWN + first_, size)
                        wait_for(res.at[h, span], br.at[m, 0])
                        edge_wait(h, span, br.at[m, 1])

    def low(p0, p1):
        return jnp.where(left, p0, pltpu.roll(p1, CELLS // 2, 1))

    def high(p0, p1):
        return jnp.where(left, pltpu.roll(p0, CELLS // 2, 1), p1)

    def rows_box(h, plane):
        x = res[h, plane]
        total = x + jnp.concatenate([edge[0, h, plane], edge[1, h, plane]], axis=0)
        for k in range(1, 4):
            total = total + jnp.where(sub >= k, pltpu.roll(x, k, 0), 0.0)
            total = total + jnp.where(sub < LOOKS - k, pltpu.roll(x, LOOKS - k, 0), 0.0)
        return total

    def cells_box(x):
        total = x
        for k in range(1, 4):
            total = total + jnp.where(lane8 >= k, pltpu.roll(x, k, 1), 0.0)
            total = total + jnp.where(lane8 < CELLS - k, pltpu.roll(x, CELLS - k, 1), 0.0)
        return total

    def ref_boxes():
        for j in range(2):
            r0, r1 = rows_box(0, 5 + j), rows_box(1, 5 + j)
            box_ref[j] = cells_box(jnp.where(c == 0, low(r0, r1), high(r0, r1)))

    def coherences(step):
        for core in range(2):

            @pl.when(c == core)
            def _():
                for j, off, place, sec, half in finals(core, step):
                    p0, p1 = res[0, place[0]], res[1, place[1]]
                    every_ifg[j, off - 1, 0] = low(p0, p1)
                    every_ifg[j, off - 1, 1] = high(p0, p1)
                    b0, b1 = rows_box(0, place[0]), rows_box(1, place[1])
                    s0, s1 = rows_box(0, sec[0]), rows_box(1, sec[1])
                    box_r, box_i = cells_box(low(b0, b1)), cells_box(high(b0, b1))
                    box_s = cells_box(high(s0, s1) if half else low(s0, s1))
                    top = jnp.sqrt(box_r * box_r + box_i * box_i)
                    every_coh[j, off - 1] = top / jnp.sqrt(box_ref[j] * box_s)

    own_copy.wait()
    second_copy.wait()
    count_copy.wait()
    chosen = []
    for j in range(2):
        for slot in range(SLOTS):
            off = jnp.clip(second[j, slot] - (4 * q + 2 * c + j), 1, OFFS)
            chosen.append((j, slot, off - 1, slot < count[j]))
    swap.wait_recv()
    for a in range(4):
        reorder(0, a, None)
    compute(0)
    all_sends(0, start)
    swap.wait_send()
    for stage in range(1, 5):
        b, a = by_core(NEXT[stage - 1]), by_core(PREV[stage - 1])
        if stage < 4:
            get_tile(1, b, None)
            get_tile(-1, a, None)
            compute(stage)
            all_sends(stage, start)
        else:
            own, far = planes_of(4, True, False), planes_of(4, False, True)
            get_tile(1, b, 0)
            own_out = looked(own, 0, 0)
            get_tile(-1, a, 0)
            far_out = looked(far, 6, 0)
            get_tile(1, b, 1)
            put_own(4, as_planes(own_out + looked(own, 0, 1)))
            own_sends(4, start)
            get_tile(-1, a, 1)
            put_far(4, as_planes(far_out + looked(far, 6, 1)))
            back_sends(4, start)
        if stage == 1:
            pass_on(0)
        if stage == 2:
            pass_on(1)
            pass_on(2)
        all_sends(stage - 1, wait_send)
        own_arrivals(stage - 1)
        if stage == 1:
            ref_boxes()
            coherences(0)
        if stage == 3:
            coherences(1)
    tile_sends(wait_send)
    for n in range(3):
        passed_on(n)
    back_arrivals(3)
    coherences(3)
    own_arrivals(4)
    coherences(2)
    back_arrivals(4)
    coherences(4)

    zero = jnp.zeros((LOOKS, CELLS), F32)
    for j, slot, off, used in chosen:
        for part in range(2):
            ifg[j, slot, part] = jnp.where(used, every_ifg[j, off, part], zero)
        coh[j, slot] = jnp.where(used, every_coh[j, off], zero)

    all_sends(4, wait_send)


def store_kernel(ifg, coh, ifg_out, coh_out, sems):
    copies = [
        pltpu.make_async_copy(ifg, ifg_out, sems.at[0]),
        pltpu.make_async_copy(coh, coh_out, sems.at[1]),
    ]
    for copy in copies:
        copy.start()
    for copy in copies:
        copy.wait()


def shards(slc, pair_second, pair_count):
    dma = pltpu.SemaphoreType.DMA
    hbm = pl.BlockSpec(memory_space=pltpu.HBM)
    vmem = pl.BlockSpec(memory_space=pltpu.VMEM)
    ifg_shape = (2, SLOTS, 2, LOOKS, CELLS)
    coh_shape = (2, SLOTS, LOOKS, CELLS)
    operands = [pltpu.with_memory_space_constraint(x, pltpu.HBM) for x in (slc, pair_second, pair_count)]
    ifg, coh = pl.pallas_call(
        planes_kernel,
        out_shape=(pltpu.VMEM(ifg_shape, F32), pltpu.VMEM(coh_shape, F32)),
        in_specs=[hbm, hbm, hbm],
        out_specs=(vmem, vmem),
        scratch_shapes=[
            pltpu.VMEM((2, N_PLANES, LOOKS, CELLS), F32),
            pltpu.VMEM((2, 2, N_PLANES, 4, CELLS), F32),
            pltpu.VMEM((3, 4, 2, ROWS, HALF), BF16),
            pltpu.VMEM((3, 4, 2, ROWS, HALF), F32),
            pltpu.VMEM((10, LOOKS, WIDTH), F32),
            pltpu.VMEM((WIDTH, CELLS), BF16),
            pltpu.VMEM((N_BACK, LOOKS, CELLS), F32),
            pltpu.VMEM((2, N_OWN, 4, CELLS), F32),
            pltpu.VMEM((2, N_BACK, 4, CELLS), F32),
            pltpu.SMEM((2, SLOTS), jnp.int32),
            pltpu.SMEM((2,), jnp.int32),
            pltpu.VMEM((2, OFFS, 2, LOOKS, CELLS), F32),
            pltpu.VMEM((2, OFFS, LOOKS, CELLS), F32),
            pltpu.VMEM((2, LOOKS, CELLS), F32),
            pltpu.SemaphoreType.REGULAR,
            dma,
            dma((2,)),
            dma,
            dma,
            dma((2, 2)),
            dma((4,)),
            dma((2, 2)),
            dma((4,)),
            dma,
            dma((4,)),
            dma,
            dma((4,)),
            dma((3,)),
            dma((5,)),
            dma((5,)),
            dma((5, 2, 2)),
            dma((5,)),
            dma((8, 3)),
            dma((8, 2)),
        ],
        compiler_params=pltpu.CompilerParams(
            collective_id=0, has_side_effects=True, vmem_limit_bytes=40 * 2**20
        ),
    )(*operands)
    return pl.pallas_call(
        store_kernel,
        out_shape=(jax.ShapeDtypeStruct(ifg_shape, F32), jax.ShapeDtypeStruct(coh_shape, F32)),
        in_specs=[vmem, vmem],
        out_specs=(pl.BlockSpec(memory_space=pl.ANY), pl.BlockSpec(memory_space=pl.ANY)),
        scratch_shapes=[dma((2,))],
        compiler_params=pltpu.CompilerParams(vmem_limit_bytes=16 * 2**20),
    )(ifg, coh)


def solution(mesh):
    in_specs = (P("date", None, "strip", None), P("date", None), P("date"))
    out_specs = (P("date", None, None, "strip", None), P("date", None, "strip", None))
    return jax.shard_map(shards, mesh=mesh, in_specs=in_specs, out_specs=out_specs, check_vma=False)
```

```python
import jax
import jax.numpy as jnp
from jax import lax
from jax.experimental import pallas as pl
from jax.experimental.pallas import tpu as pltpu
from jax.sharding import PartitionSpec as P

MESH = pl.DeviceIdType.MESH
F32 = jnp.float32
BF16 = jnp.bfloat16

LOOK_AZ = 5
LOOK_RG = 20
SLOTS = 6
OFFS = 8
CHIPS = 16
STRIPS = 8
ROWS = 40
WIDTH = 2560
HALF = WIDTH // 2
LOOKS = ROWS // LOOK_AZ
CELLS = 128
PLANE_SCALE = 1.0 / (LOOK_AZ * LOOK_RG)


def pair(a, b):
    return ("pair", a, b)


def power(a, b):
    return ("power", a, b)


def onto(b, *middle):
    return [pair((0, 0), (1, b)), pair((0, 1), (1, b)), *middle, pair((0, 2), (1, b)), pair((0, 3), (1, b))]


NEXT = [(0, 2), (2, 0), (1, 3), (3, 1)]
PREV = [(1, 3), (3, 1), (0, 2), (2, 0)]
SAME = [(0, 1), (0, 2), (0, 3), (1, 2), (1, 3)]
STAGES = [
    [pair((0, a), (0, b)) for a, b in SAME] + [power((0, 0), (0, 2)), power((0, 1), (0, 3)), pair((0, 2), (0, 3))],
    onto(NEXT[0]),
    onto(NEXT[1], power((1, 0), (1, 2))),
    onto(NEXT[2]),
    onto(NEXT[3], power((1, 1), (1, 3))),
]
STARTS = [0, 8, 12, 17, 21]
NEEDS = [[(0, 7), (5, 3)], [(0, 2), (2, 2)], [(0, 3), (2, 3)], [(0, 2), (2, 2)], [(0, 3), (2, 3)]]
N_OWN = 26
IA, IB = 14, 23
BACK = [
    [],
    [(((1, 0), 0), ((3, 2), 2))],
    [(((3, 0), 4), ((3, 0), 3)), (((3, 2), 5), ((1, 0), 0))],
    [(((0, 0), 1), ((3, 3), 4)), (((1, 1), 2), ((2, 0), 5)), (((3, 1), 6), ((2, 2), 6))],
    [(((2, 0), 10), ((3, 1), 12)), (((2, 2), 11), ((2, 1), 13)), (((2, 1), 12), ((1, 1), 9)), (((3, 3), 13), ((0, 0), 10))],
]
BACK_POWER = {2: [(3, 7), (1, 7)], 4: [(8, 9), (8, 11)]}
N_BACK = 14
BACK_SENDS = [
    (3, 0, 0, 0, 4),
    (3, 0, 1, 4, 4),
    (3, 1, 0, 0, 2),
    (3, 1, 1, 2, 6),
    (4, 0, 0, 8, 1),
    (4, 0, 1, 9, 5),
    (4, 1, 0, 8, 3),
    (4, 1, 1, 11, 3),
]
FAR = [{}, {}]
for stage_ in BACK:
    for both_ in stage_:
        for core_ in range(2):
            FAR[core_][both_[core_][0]] = both_[core_][1]
N_PLANES = N_OWN + N_BACK


def arrival(b, core):
    return 1 + [x[core] for x in NEXT].index(b)


def finals(core, when_):
    found = []
    for j in range(2):
        a = 2 * core + j
        for off in range(1, OFFS + 1):
            chip, e = divmod(a + off, 4)
            odd, half = e % 2, e // 2
            if chip == 0:
                step, place = 0, [(SAME + [None, None, (2, 3)]).index((a, e))] * 2
                sec = [6 if odd else 5] * 2
            elif chip == 1:
                step, place = 2 if odd else 1, []
                for h in range(2):
                    t = arrival(e, h)
                    place.append(STARTS[t] + a + (1 if t % 2 == 0 and a >= 2 else 0))
                sec = [IB if odd else IA] * 2
            else:
                place = [N_OWN + FAR[h][(a, e)] for h in range(2)]
                late = any(spec[0] == 4 and spec[1] == h and spec[3] <= FAR[h][(a, e)] < spec[3] + spec[4] for spec in BACK_SENDS for h in range(2))
                step = 4 if late or odd else 3
                sec = [N_OWN + BACK_POWER[4 if odd else 2][h][core] for h in range(2)]
            if step == when_:
                found.append((j, off, place, sec, half))
    return found


def when(*conditions):
    conditions = [x for x in conditions if x is not None]
    if not conditions:
        return lambda f: f()
    total = conditions[0]
    for x in conditions[1:]:
        total = jnp.logical_and(total, x)
    return pl.when(total)


def planes_kernel(
    slc, second_in, count_in, ifg, coh, res, edge, tiles, looks, sums, table, back, rim, back_rim, second, count, every_ifg, every_coh, box_ref,
    ready, lsem, sem2, xs, xr, us, ur, vs, vr, us2, ur2, vs2, vr2, fs, ps, pr, hs, hr, bs, br,
):
    date = lax.axis_index("date")
    strip = lax.axis_index("strip")
    q = date // 2
    c = date % 2
    other = 1 - c
    has_prev, has_next = q > 0, q < CHIPS - 1
    has_up, has_down = strip > 0, strip < STRIPS - 1

    def device(dq, core, ds):
        return ((q + dq) * 2 + core, strip + ds)

    def side_ok(ds):
        return {0: None, -1: has_up, 1: has_down}[ds]

    def chip_ok(dq):
        return {0: None, -1: has_prev, 1: has_next}[dq]

    def by_core(x):
        if isinstance(x, tuple):
            return jnp.where(c == 0, x[0], x[1])
        return x

    barrier = pltpu.get_barrier_semaphore()
    last, mid = CHIPS - 1, CHIPS // 2

    def hello(semaphore, chip, core, row):
        pl.semaphore_signal(semaphore, inc=1, device_id=(chip * 2 + core, row), device_id_type=MESH)

    def hello_both(semaphore, chip):
        for core in range(2):
            hello(semaphore, chip, core, strip)

    pl.when(q == 0)(lambda: hello_both(barrier, mid))
    pl.when(q == mid - 1)(lambda: hello_both(barrier, last))

    def waits_apart(chip):
        return jnp.logical_and(chip % 8 >= 3, chip % 8 <= 3)

    when(has_prev, jnp.logical_not(waits_apart(q - 1)))(lambda: hello_both(barrier, q - 1))
    when(has_next, q != mid - 1)(lambda: hello_both(barrier, q + 1))
    when(has_up)(lambda: hello(barrier, q, c, strip - 1))
    when(has_down)(lambda: hello(barrier, q, c, strip + 1))
    hello(barrier, q, other, strip)

    own_copy = pltpu.make_async_copy(
        slc.at[:, :, :, pl.ds(pl.multiple_of(c * HALF, HALF), HALF)], tiles.at[1, pl.ds(2 * c, 2)], lsem
    )
    own_copy.start()
    second_copy = pltpu.make_async_copy(second_in, second, sem2.at[0])
    count_copy = pltpu.make_async_copy(count_in, count, sem2.at[1])
    second_copy.start()
    count_copy.start()

    def as_int(x):
        return jnp.where(x, 1, 0)

    apart = jnp.logical_and(has_next, waits_apart(q))
    greeted = 1 + 2 * (as_int(has_prev) + as_int(has_next) - as_int(apart) - as_int(q == mid)) + as_int(has_up) + as_int(has_down)
    pl.semaphore_wait(barrier, greeted + 2 * as_int(jnp.logical_or(q == mid, q == last)))
    when(has_prev, waits_apart(q - 1))(lambda: hello_both(ready, q - 1))
    pl.when(q == last)(lambda: hello_both(ready, mid - 1))
    pl.when(q == mid - 1)(lambda: hello_both(ready, mid))

    swap = pltpu.make_async_remote_copy(
        src_ref=slc.at[:, :, :, pl.ds(pl.multiple_of(other * HALF, HALF), HALF)],
        dst_ref=tiles.at[1, pl.ds(2 * c, 2)],
        send_sem=xs,
        recv_sem=xr,
        device_id=device(0, other, 0),
        device_id_type=MESH,
    )

    PASSED = {-1: [(2, None), (3, 1)], 1: [(2, None)]}

    def tile_copy(dq, j, core, relay, part):
        send, recv = (us.at[j, core], ur) if dq < 0 else (vs.at[j, core], vr)
        if part == 1:
            send = us2 if dq < 0 else vs2
        chip = q + dq
        if relay:
            chip = 0 if dq < 0 else last
        if relay:
            recv = vr if dq < 0 else ur
        if part == 1:
            recv = {0: ur2, 1: vr2}[0 if recv is ur else 1]
        start_, width = (0, HALF) if part is None else (part * HALF // 2, HALF // 2)
        return pltpu.make_async_remote_copy(
            src_ref=slc.at[j, :, :, pl.ds(core * HALF + start_, width)],
            dst_ref=tiles.at[1 + dq if relay else 1 - dq, 2 * c + j, :, :, pl.ds(start_, width)],
            send_sem=send,
            recv_sem=recv.at[2 * c + j],
            device_id=(chip * 2 + core, strip),
            device_id_type=MESH,
        )

    def part_of(ref, part):
        if part is None:
            return ref
        return ref.at[:, :, pl.ds(part * HALF // 2, HALF // 2)]

    def forward_copy(n, at_first):
        which, part = PASSED[-1 if at_first else 1][n]
        step = which - 2
        a = by_core((NEXT if at_first else PREV)[2 + step])
        side = 2 if at_first else 0
        came, recv = (vr, ur) if at_first else (ur, vr)
        if part == 1:
            came, recv = (vr2, ur2) if at_first else (ur2, vr2)
        here = part_of(tiles.at[2 - side, a], part)
        copy = pltpu.make_async_remote_copy(
            src_ref=here,
            dst_ref=part_of(tiles.at[side, a], part),
            send_sem=fs.at[n],
            recv_sem=recv.at[a],
            device_id=((mid - 1 if at_first else mid) * 2 + c, strip),
            device_id_type=MESH,
        )
        return here, came.at[a], copy

    def pass_on(n):
        def one(at_first):
            here, came, copy = forward_copy(n, at_first)
            pltpu.make_async_copy(here, here, came).wait()
            copy.start()

        if n < len(PASSED[-1]):
            pl.when(q == 0)(lambda: one(True))
        if n < len(PASSED[1]):
            pl.when(q == last)(lambda: one(False))

    def passed_on(n):
        if n < len(PASSED[-1]):
            pl.when(q == 0)(lambda: forward_copy(n, True)[2].wait_send())
        if n < len(PASSED[1]):
            pl.when(q == last)(lambda: forward_copy(n, False)[2].wait_send())

    def tile_sends(act, times=(0, 1)):
        for here in range(2):

            @pl.when(c == here)
            def _():
                for n in range(4):
                    for dq in (-1, 1):
                        j = n // 2 if dq < 0 else 1 - n // 2
                        core = (here + n) % 2

                        far = q == (mid if dq < 0 else mid - 1)

                        def send_parts(relay):
                            for part in (0, 1) if n == 3 else (None,):
                                if relay is None or relay == ((n, part) in PASSED[dq]):
                                    act(tile_copy(dq, j, core, bool(relay), part))

                        for time in times:
                            if dq < 0:
                                if time == 0:
                                    when(has_prev, jnp.logical_not(far))(lambda: send_parts(None))
                                else:
                                    when(far)(lambda: send_parts(False))
                                    when(far)(lambda: send_parts(True))
                            else:
                                waiting = apart if time == 1 else jnp.logical_not(apart)
                                when(has_next, waiting, jnp.logical_not(far))(lambda: send_parts(None))
                                when(far)(lambda: send_parts(time == 1))

    def start(copy):
        copy.start()

    def wait_send(copy):
        copy.wait_send()

    tile_sends(start, (0,))
    swap.start()

    first = lax.broadcasted_iota(jnp.int32, (CELLS, CELLS), 1) * LOOK_RG
    lane = lax.broadcasted_iota(jnp.int32, (CELLS, CELLS), 0)

    def fill(i, carry):
        delta = lane + i * CELLS - first
        inside = jnp.logical_and(delta >= 0, delta < LOOK_RG)
        table[pl.ds(pl.multiple_of(i * CELLS, CELLS), CELLS), :] = jnp.where(inside, 1.0, 0.0).astype(BF16)
        return carry

    lax.fori_loop(0, WIDTH // CELLS, fill, 0)

    @pl.when(jnp.logical_or(apart, jnp.logical_or(q == mid - 1, q == mid)))
    def _():
        pl.semaphore_wait(ready, 2)
        tile_sends(start, (1,))

    row = lax.broadcasted_iota(jnp.int32, (ROWS, ROWS), 0)
    col = lax.broadcasted_iota(jnp.int32, (ROWS, ROWS), 1)
    order = jnp.where(col == LOOK_AZ * (row % LOOKS) + row // LOOKS, 1.0, 0.0).astype(BF16)
    sub = lax.broadcasted_iota(jnp.int32, (LOOKS, CELLS), 0)
    lane8 = lax.broadcasted_iota(jnp.int32, (LOOKS, CELLS), 1)
    left = lane8 < CELLS // 2

    @pl.when(jnp.logical_not(has_up))
    def _():
        edge[0] = jnp.zeros(edge.shape[1:], F32)

    @pl.when(jnp.logical_not(has_down))
    def _():
        edge[1] = jnp.zeros(edge.shape[1:], F32)

    def get_tile(rel, a, part):
        @when(chip_ok(rel))
        def _():
            whole, second_half = (ur, ur2) if rel > 0 else (vr, vr2)
            ref = part_of(tiles.at[1 + rel, a], part)
            pltpu.make_async_copy(ref, ref, (second_half if part == 1 else whole).at[a]).wait()
            reorder(rel, a, part)

    def reorder(rel, a, part):
        at = slice(None) if part is None else pl.ds(part * HALF // 2, HALF // 2)
        for i in range(2):
            looks[1 + rel, a, i, :, at] = jnp.dot(order, tiles[1 + rel, a, i, :, at], preferred_element_type=F32)

    def rims(x):
        d = jnp.where(sub < 3, pltpu.roll(x, 3, 0), 0.0)
        d = d + pltpu.roll(d, LOOKS - 1, 0) + pltpu.roll(d, LOOKS - 2, 0)
        u = jnp.where(jnp.logical_and(sub >= 1, sub < 4), pltpu.roll(x, 1, 0), 0.0)
        u = u + pltpu.roll(u, 1, 0) + pltpu.roll(u, 2, 0)
        return d[0:4], u[0:4]

    def planes_of(stage, own, far):
        planes = list(STAGES[stage]) if own else []
        if far:
            for (pair0, _), (pair1, _) in BACK[stage]:
                planes.append(pair((-1, (pair0[0], pair1[0])), (1, (pair0[1], pair1[1]))))
        return [(kind, (u[0], by_core(u[1])), (v[0], by_core(v[1]))) for kind, u, v in planes]

    def looked(planes, at0, part):
        n = len(planes)
        m = n + n % 2

        def lanes(t, carry):
            at = pl.ds(pl.multiple_of(t * CELLS, CELLS), CELLS)
            at2 = pl.ds(pl.multiple_of(t * CELLS + HALF, CELLS), CELLS)

            def total(x):
                return jnp.sum(x.reshape(LOOK_AZ, LOOKS, CELLS), axis=0)

            for i, (kind, u, v) in enumerate(planes):
                u_r, u_i = looks[1 + u[0], u[1], 0, :, at], looks[1 + u[0], u[1], 1, :, at]
                v_r, v_i = looks[1 + v[0], v[1], 0, :, at], looks[1 + v[0], v[1], 1, :, at]
                if kind == "pair":
                    x, y = u_r * v_r + u_i * v_i, u_i * v_r - u_r * v_i
                else:
                    x, y = u_r * u_r + u_i * u_i, v_r * v_r + v_i * v_i
                sums[at0 + i, :, at] = total(x)
                sums[at0 + i, :, at2] = total(y)
            return carry

        steps = HALF // CELLS
        spans = [(0, WIDTH)]
        first_, end = 0, steps
        if part is not None:
            spans = [(part * HALF // 2, HALF // 2), (HALF + part * HALF // 2, HALF // 2)]
            first_, end = part * steps // 2, (part + 1) * steps // 2
        lax.fori_loop(first_, end, lanes, 0)
        if m > n:
            sums[at0 + n] = jnp.zeros((LOOKS, WIDTH), F32)
        out = None
        for at, width in spans:
            x = sums[at0 : at0 + m, :, at : at + width].reshape(m * LOOKS, width)
            hi = x.astype(BF16)
            lo = (x - hi.astype(F32)).astype(BF16)
            t = table[at : at + width, :]
            both = jnp.dot(jnp.concatenate([hi, lo], axis=0), t, preferred_element_type=F32)
            y = both[0 : m * LOOKS] + both[m * LOOKS :]
            out = y if out is None else out + y
        return out

    def as_planes(out):
        return (out * PLANE_SCALE).reshape(out.shape[0] // LOOKS, LOOKS, CELLS)

    def put_back(places, out):
        for i, place in places:
            place = by_core(place)
            back[place] = out[i]
            back_rim[0, place], back_rim[1, place] = rims(out[i])

    def put_own(stage, out):
        for i in range(len(STAGES[stage])):
            res[c, STARTS[stage] + i] = out[i]
            rim[0, STARTS[stage] + i], rim[1, STARTS[stage] + i] = rims(out[i])
        if stage in BACK_POWER:
            put_back([(2, both) for both in zip(*BACK_POWER[stage], strict=True)], out)

    def put_far(stage, out):
        put_back([(i, (p0, p1)) for i, ((_, p0), (_, p1)) in enumerate(BACK[stage])], out)

    def compute(stage):
        out = as_planes(looked(planes_of(stage, True, True), 0, None))
        put_own(stage, out)
        put_far(stage, out[len(STAGES[stage]) :])

    def span_of(stage, core):
        if stage == 0:
            return pl.ds(0, 8)
        return pl.ds(STARTS[stage] + 2 * core, NEEDS[stage][0][1])

    def core_send(stage):
        return pltpu.make_async_remote_copy(
            src_ref=res.at[c, span_of(stage, other)],
            dst_ref=res.at[c, span_of(stage, other)],
            send_sem=ps.at[stage],
            recv_sem=pr.at[stage],
            device_id=device(0, other, 0),
            device_id_type=MESH,
        )

    def rim_send(stage, core, ds):
        first_, size = NEEDS[stage][core]
        side = (1 - ds) // 2
        span = pl.ds(STARTS[stage] + first_, size)
        return pltpu.make_async_remote_copy(
            src_ref=rim.at[side, span],
            dst_ref=edge.at[side, c, span],
            send_sem=hs.at[stage, core, side],
            recv_sem=hr.at[stage],
            device_id=device(0, core, ds),
            device_id_type=MESH,
        )

    def back_send(m, ds):
        _, _, core, first_, size = BACK_SENDS[m]
        span, there = pl.ds(first_, size), pl.ds(N_OWN + first_, size)
        if ds == 0:
            src, dst = back.at[span], res.at[c, there]
        else:
            side = (1 - ds) // 2
            src, dst = back_rim.at[side, span], edge.at[side, c, there]
        return pltpu.make_async_remote_copy(
            src_ref=src,
            dst_ref=dst,
            send_sem=bs.at[m, 1 + ds],
            recv_sem=br.at[m, 0 if ds == 0 else 1],
            device_id=device(-1, core, ds),
            device_id_type=MESH,
        )

    def back_sends(stage, act):
        for here in range(2):
            specs = [m for m, spec in enumerate(BACK_SENDS) if spec[0] == stage and spec[1] == here]
            if specs:

                @when(c == here, has_prev)
                def _():
                    for ds in (-1, 1, 0):

                        @when(side_ok(ds))
                        def _():
                            for m in specs:
                                act(back_send(m, ds))

    def own_sends(stage, act):
        for ds in (-1, 1):

            @when(side_ok(ds))
            def _():
                for core in range(2):
                    act(rim_send(stage, core, ds))

        act(core_send(stage))

    def all_sends(stage, act):
        back_sends(stage, act)
        own_sends(stage, act)

    def wait_for(ref, sem):
        pltpu.make_async_copy(ref, ref, sem).wait()

    def edge_wait(h, span, sem):
        here = edge if h is None else edge.at[:, pl.ds(h, 1)]
        when(has_up, has_down)(lambda: wait_for(here.at[:, :, span], sem))
        when(jnp.logical_not(has_up))(lambda: wait_for(here.at[1, :, span], sem))
        when(jnp.logical_not(has_down))(lambda: wait_for(here.at[0, :, span], sem))

    def own_arrivals(stage):
        wait_for(res.at[other, span_of(stage, c)], pr.at[stage])
        if stage == 0:
            for core in range(2):
                first_, size = NEEDS[0][core]
                pl.when(c == core)(lambda: edge_wait(None, pl.ds(first_, size), hr.at[0]))
        else:
            edge_wait(None, span_of(stage, c), hr.at[stage])

    def back_arrivals(stage):
        for core in range(2):

            @when(has_next, c == core)
            def _():
                for m, (after, h, to, first_, size) in enumerate(BACK_SENDS):
                    if after == stage and to == core:
                        span = pl.ds(N_OWN + first_, size)
                        wait_for(res.at[h, span], br.at[m, 0])
                        edge_wait(h, span, br.at[m, 1])

    def low(p0, p1):
        return jnp.where(left, p0, pltpu.roll(p1, CELLS // 2, 1))

    def high(p0, p1):
        return jnp.where(left, pltpu.roll(p0, CELLS // 2, 1), p1)

    def rows_box(h, plane):
        x = res[h, plane]
        total = x + jnp.concatenate([edge[0, h, plane], edge[1, h, plane]], axis=0)
        for k in range(1, 4):
            total = total + jnp.where(sub >= k, pltpu.roll(x, k, 0), 0.0)
            total = total + jnp.where(sub < LOOKS - k, pltpu.roll(x, LOOKS - k, 0), 0.0)
        return total

    def cells_box(x):
        total = x
        for k in range(1, 4):
            total = total + jnp.where(lane8 >= k, pltpu.roll(x, k, 1), 0.0)
            total = total + jnp.where(lane8 < CELLS - k, pltpu.roll(x, CELLS - k, 1), 0.0)
        return total

    def ref_boxes():
        for j in range(2):
            r0, r1 = rows_box(0, 5 + j), rows_box(1, 5 + j)
            box_ref[j] = cells_box(jnp.where(c == 0, low(r0, r1), high(r0, r1)))

    def coherences(step):
        for core in range(2):

            @pl.when(c == core)
            def _():
                for j, off, place, sec, half in finals(core, step):
                    p0, p1 = res[0, place[0]], res[1, place[1]]
                    every_ifg[j, off - 1, 0] = low(p0, p1)
                    every_ifg[j, off - 1, 1] = high(p0, p1)
                    b0, b1 = rows_box(0, place[0]), rows_box(1, place[1])
                    s0, s1 = rows_box(0, sec[0]), rows_box(1, sec[1])
                    box_r, box_i = cells_box(low(b0, b1)), cells_box(high(b0, b1))
                    box_s = cells_box(high(s0, s1) if half else low(s0, s1))
                    top = jnp.sqrt(box_r * box_r + box_i * box_i)
                    every_coh[j, off - 1] = top / jnp.sqrt(box_ref[j] * box_s)

    own_copy.wait()
    second_copy.wait()
    count_copy.wait()
    chosen = []
    for j in range(2):
        for slot in range(SLOTS):
            off = jnp.clip(second[j, slot] - (4 * q + 2 * c + j), 1, OFFS)
            chosen.append((j, slot, off - 1, slot < count[j]))
    swap.wait_recv()
    for a in range(4):
        reorder(0, a, None)
    compute(0)
    all_sends(0, start)
    swap.wait_send()
    for stage in range(1, 5):
        b, a = by_core(NEXT[stage - 1]), by_core(PREV[stage - 1])
        if stage < 4:
            get_tile(1, b, None)
            get_tile(-1, a, None)
            compute(stage)
            all_sends(stage, start)
        else:
            own, far = planes_of(4, True, False), planes_of(4, False, True)
            get_tile(1, b, 0)
            own_out = looked(own, 0, 0)
            get_tile(-1, a, 0)
            far_out = looked(far, 6, 0)
            get_tile(1, b, 1)
            put_own(4, as_planes(own_out + looked(own, 0, 1)))
            own_sends(4, start)
            get_tile(-1, a, 1)
            put_far(4, as_planes(far_out + looked(far, 6, 1)))
            back_sends(4, start)
        if stage == 1:
            pass_on(0)
        if stage == 2:
            pass_on(1)
            pass_on(2)
        all_sends(stage - 1, wait_send)
        own_arrivals(stage - 1)
        if stage == 1:
            ref_boxes()
            coherences(0)
        if stage == 3:
            coherences(1)
    tile_sends(wait_send)
    for n in range(3):
        passed_on(n)
    back_arrivals(3)
    coherences(3)
    own_arrivals(4)
    coherences(2)
    all_sends(4, wait_send)
    back_arrivals(4)
    coherences(4)

    zero = jnp.zeros((LOOKS, CELLS), F32)
    for j, slot, off, used in chosen:
        for part in range(2):
            ifg[j, slot, part] = jnp.where(used, every_ifg[j, off, part], zero)
        coh[j, slot] = jnp.where(used, every_coh[j, off], zero)


def store_kernel(ifg, coh, ifg_out, coh_out, sems):
    copies = [
        pltpu.make_async_copy(ifg, ifg_out, sems.at[0]),
        pltpu.make_async_copy(coh, coh_out, sems.at[1]),
    ]
    for copy in copies:
        copy.start()
    for copy in copies:
        copy.wait()


def shards(slc, pair_second, pair_count):
    dma = pltpu.SemaphoreType.DMA
    hbm = pl.BlockSpec(memory_space=pltpu.HBM)
    vmem = pl.BlockSpec(memory_space=pltpu.VMEM)
    ifg_shape = (2, SLOTS, 2, LOOKS, CELLS)
    coh_shape = (2, SLOTS, LOOKS, CELLS)
    operands = [pltpu.with_memory_space_constraint(x, pltpu.HBM) for x in (slc, pair_second, pair_count)]
    ifg, coh = pl.pallas_call(
        planes_kernel,
        out_shape=(pltpu.VMEM(ifg_shape, F32), pltpu.VMEM(coh_shape, F32)),
        in_specs=[hbm, hbm, hbm],
        out_specs=(vmem, vmem),
        scratch_shapes=[
            pltpu.VMEM((2, N_PLANES, LOOKS, CELLS), F32),
            pltpu.VMEM((2, 2, N_PLANES, 4, CELLS), F32),
            pltpu.VMEM((3, 4, 2, ROWS, HALF), BF16),
            pltpu.VMEM((3, 4, 2, ROWS, HALF), F32),
            pltpu.VMEM((10, LOOKS, WIDTH), F32),
            pltpu.VMEM((WIDTH, CELLS), BF16),
            pltpu.VMEM((N_BACK, LOOKS, CELLS), F32),
            pltpu.VMEM((2, N_OWN, 4, CELLS), F32),
            pltpu.VMEM((2, N_BACK, 4, CELLS), F32),
            pltpu.SMEM((2, SLOTS), jnp.int32),
            pltpu.SMEM((2,), jnp.int32),
            pltpu.VMEM((2, OFFS, 2, LOOKS, CELLS), F32),
            pltpu.VMEM((2, OFFS, LOOKS, CELLS), F32),
            pltpu.VMEM((2, LOOKS, CELLS), F32),
            pltpu.SemaphoreType.REGULAR,
            dma,
            dma((2,)),
            dma,
            dma,
            dma((2, 2)),
            dma((4,)),
            dma((2, 2)),
            dma((4,)),
            dma,
            dma((4,)),
            dma,
            dma((4,)),
            dma((3,)),
            dma((5,)),
            dma((5,)),
            dma((5, 2, 2)),
            dma((5,)),
            dma((8, 3)),
            dma((8, 2)),
        ],
        compiler_params=pltpu.CompilerParams(
            collective_id=0, has_side_effects=True, vmem_limit_bytes=40 * 2**20
        ),
    )(*operands)
    return pl.pallas_call(
        store_kernel,
        out_shape=(jax.ShapeDtypeStruct(ifg_shape, F32), jax.ShapeDtypeStruct(coh_shape, F32)),
        in_specs=[vmem, vmem],
        out_specs=(pl.BlockSpec(memory_space=pl.ANY), pl.BlockSpec(memory_space=pl.ANY)),
        scratch_shapes=[dma((2,))],
        compiler_params=pltpu.CompilerParams(vmem_limit_bytes=16 * 2**20),
    )(ifg, coh)


def solution(mesh):
    in_specs = (P("date", None, "strip", None), P("date", None), P("date"))
    out_specs = (P("date", None, None, "strip", None), P("date", None, "strip", None))
    return jax.shard_map(shards, mesh=mesh, in_specs=in_specs, out_specs=out_specs, check_vma=False)
```

```python
import jax
import jax.numpy as jnp
from jax import lax
from jax.experimental import pallas as pl
from jax.experimental.pallas import tpu as pltpu
from jax.sharding import PartitionSpec as P

MESH = pl.DeviceIdType.MESH
F32 = jnp.float32
BF16 = jnp.bfloat16

LOOK_AZ = 5
LOOK_RG = 20
SLOTS = 6
OFFS = 8
CHIPS = 16
STRIPS = 8
ROWS = 40
WIDTH = 2560
HALF = WIDTH // 2
LOOKS = ROWS // LOOK_AZ
CELLS = 128
PLANE_SCALE = 1.0 / (LOOK_AZ * LOOK_RG)


def pair(a, b):
    return ("pair", a, b)


def power(a, b):
    return ("power", a, b)


def onto(b, *middle):
    return [pair((0, 0), (1, b)), pair((0, 1), (1, b)), *middle, pair((0, 2), (1, b)), pair((0, 3), (1, b))]


NEXT = [(0, 2), (2, 0), (1, 3), (3, 1)]
PREV = [(1, 3), (3, 1), (0, 2), (2, 0)]
SAME = [(0, 1), (0, 2), (0, 3), (1, 2), (1, 3)]
STAGES = [
    [pair((0, a), (0, b)) for a, b in SAME] + [power((0, 0), (0, 2)), power((0, 1), (0, 3)), pair((0, 2), (0, 3))],
    onto(NEXT[0]),
    onto(NEXT[1], power((1, 0), (1, 2))),
    onto(NEXT[2]),
    onto(NEXT[3], power((1, 1), (1, 3))),
]
STARTS = [0, 8, 12, 17, 21]
NEEDS = [[(0, 7), (5, 3)], [(0, 2), (2, 2)], [(0, 3), (2, 3)], [(0, 2), (2, 2)], [(0, 3), (2, 3)]]
N_OWN = 26
IA, IB = 14, 23
BACK = [
    [],
    [(((1, 0), 0), ((3, 2), 2))],
    [(((3, 0), 4), ((3, 0), 3)), (((3, 2), 5), ((1, 0), 0))],
    [(((0, 0), 1), ((3, 3), 4)), (((1, 1), 2), ((2, 0), 5)), (((3, 1), 6), ((2, 2), 6))],
    [(((2, 0), 10), ((3, 1), 12)), (((2, 2), 11), ((2, 1), 13)), (((2, 1), 12), ((1, 1), 9)), (((3, 3), 13), ((0, 0), 10))],
]
BACK_POWER = {2: [(3, 7), (1, 7)], 4: [(8, 9), (8, 11)]}
N_BACK = 14
BACK_SENDS = [
    (3, 0, 0, 0, 4),
    (3, 0, 1, 4, 4),
    (3, 1, 0, 0, 2),
    (3, 1, 1, 2, 6),
    (4, 0, 0, 8, 1),
    (4, 0, 1, 9, 5),
    (4, 1, 0, 8, 3),
    (4, 1, 1, 11, 3),
]
FAR = [{}, {}]
for stage_ in BACK:
    for both_ in stage_:
        for core_ in range(2):
            FAR[core_][both_[core_][0]] = both_[core_][1]
N_PLANES = N_OWN + N_BACK


def arrival(b, core):
    return 1 + [x[core] for x in NEXT].index(b)


def finals(core, when_):
    found = []
    for j in range(2):
        a = 2 * core + j
        for off in range(1, OFFS + 1):
            chip, e = divmod(a + off, 4)
            odd, half = e % 2, e // 2
            if chip == 0:
                step, place = 0, [(SAME + [None, None, (2, 3)]).index((a, e))] * 2
                sec = [6 if odd else 5] * 2
            elif chip == 1:
                step, place = 2 if odd else 1, []
                for h in range(2):
                    t = arrival(e, h)
                    place.append(STARTS[t] + a + (1 if t % 2 == 0 and a >= 2 else 0))
                sec = [IB if odd else IA] * 2
            else:
                place = [N_OWN + FAR[h][(a, e)] for h in range(2)]
                late = any(spec[0] == 4 and spec[1] == h and spec[3] <= FAR[h][(a, e)] < spec[3] + spec[4] for spec in BACK_SENDS for h in range(2))
                step = 4 if late or odd else 3
                sec = [N_OWN + BACK_POWER[4 if odd else 2][h][core] for h in range(2)]
            if step == when_:
                found.append((j, off, place, sec, half))
    return found


def when(*conditions):
    conditions = [x for x in conditions if x is not None]
    if not conditions:
        return lambda f: f()
    total = conditions[0]
    for x in conditions[1:]:
        total = jnp.logical_and(total, x)
    return pl.when(total)


def planes_kernel(
    slc, second_in, count_in, ifg, coh, res, edge, tiles, looks, sums, table, back, rim, back_rim, second, count, every_ifg, every_coh, box_ref,
    ready, lsem, sem2, xs, xr, us, ur, vs, vr, us2, ur2, vs2, vr2, fs, ps, pr, hs, hr, bs, br,
):
    date = lax.axis_index("date")
    strip = lax.axis_index("strip")
    q = date // 2
    c = date % 2
    other = 1 - c
    has_prev, has_next = q > 0, q < CHIPS - 1
    has_up, has_down = strip > 0, strip < STRIPS - 1

    def device(dq, core, ds):
        return ((q + dq) * 2 + core, strip + ds)

    def side_ok(ds):
        return {0: None, -1: has_up, 1: has_down}[ds]

    def chip_ok(dq):
        return {0: None, -1: has_prev, 1: has_next}[dq]

    def by_core(x):
        if isinstance(x, tuple):
            return jnp.where(c == 0, x[0], x[1])
        return x

    barrier = pltpu.get_barrier_semaphore()
    last, mid = CHIPS - 1, CHIPS // 2

    def hello(semaphore, chip, core, row):
        pl.semaphore_signal(semaphore, inc=1, device_id=(chip * 2 + core, row), device_id_type=MESH)

    def hello_both(semaphore, chip):
        for core in range(2):
            hello(semaphore, chip, core, strip)

    when(has_up)(lambda: hello(barrier, q, c, strip - 1))
    when(has_down)(lambda: hello(barrier, q, c, strip + 1))
    pl.when(q == 0)(lambda: hello_both(barrier, mid))
    pl.when(q == mid - 1)(lambda: hello_both(barrier, last))

    def waits_apart(chip):
        return jnp.logical_and(chip % 8 >= 3, chip % 8 <= 3)

    when(has_prev, jnp.logical_not(waits_apart(q - 1)))(lambda: hello_both(barrier, q - 1))
    when(has_next, q != mid - 1)(lambda: hello_both(barrier, q + 1))
    hello(barrier, q, other, strip)

    own_copy = pltpu.make_async_copy(
        slc.at[:, :, :, pl.ds(pl.multiple_of(c * HALF, HALF), HALF)], tiles.at[1, pl.ds(2 * c, 2)], lsem
    )
    own_copy.start()
    second_copy = pltpu.make_async_copy(second_in, second, sem2.at[0])
    count_copy = pltpu.make_async_copy(count_in, count, sem2.at[1])
    second_copy.start()
    count_copy.start()

    def as_int(x):
        return jnp.where(x, 1, 0)

    apart = jnp.logical_and(has_next, waits_apart(q))
    greeted = 1 + 2 * (as_int(has_prev) + as_int(has_next) - as_int(apart) - as_int(q == mid)) + as_int(has_up) + as_int(has_down)
    pl.semaphore_wait(barrier, greeted + 2 * as_int(jnp.logical_or(q == mid, q == last)))
    when(has_prev, waits_apart(q - 1))(lambda: hello_both(ready, q - 1))
    pl.when(q == last)(lambda: hello_both(ready, mid - 1))
    pl.when(q == mid - 1)(lambda: hello_both(ready, mid))

    swap = pltpu.make_async_remote_copy(
        src_ref=slc.at[:, :, :, pl.ds(pl.multiple_of(other * HALF, HALF), HALF)],
        dst_ref=tiles.at[1, pl.ds(2 * c, 2)],
        send_sem=xs,
        recv_sem=xr,
        device_id=device(0, other, 0),
        device_id_type=MESH,
    )

    PASSED = {-1: [(2, None), (3, 1)], 1: [(2, None)]}

    def tile_copy(dq, j, core, relay, part):
        send, recv = (us.at[j, core], ur) if dq < 0 else (vs.at[j, core], vr)
        if part == 1:
            send = us2 if dq < 0 else vs2
        chip = q + dq
        if relay:
            chip = 0 if dq < 0 else last
        if relay:
            recv = vr if dq < 0 else ur
        if part == 1:
            recv = {0: ur2, 1: vr2}[0 if recv is ur else 1]
        start_, width = (0, HALF) if part is None else (part * HALF // 2, HALF // 2)
        return pltpu.make_async_remote_copy(
            src_ref=slc.at[j, :, :, pl.ds(core * HALF + start_, width)],
            dst_ref=tiles.at[1 + dq if relay else 1 - dq, 2 * c + j, :, :, pl.ds(start_, width)],
            send_sem=send,
            recv_sem=recv.at[2 * c + j],
            device_id=(chip * 2 + core, strip),
            device_id_type=MESH,
        )

    def part_of(ref, part):
        if part is None:
            return ref
        return ref.at[:, :, pl.ds(part * HALF // 2, HALF // 2)]

    def forward_copy(n, at_first):
        which, part = PASSED[-1 if at_first else 1][n]
        step = which - 2
        a = by_core((NEXT if at_first else PREV)[2 + step])
        side = 2 if at_first else 0
        came, recv = (vr, ur) if at_first else (ur, vr)
        if part == 1:
            came, recv = (vr2, ur2) if at_first else (ur2, vr2)
        here = part_of(tiles.at[2 - side, a], part)
        copy = pltpu.make_async_remote_copy(
            src_ref=here,
            dst_ref=part_of(tiles.at[side, a], part),
            send_sem=fs.at[n],
            recv_sem=recv.at[a],
            device_id=((mid - 1 if at_first else mid) * 2 + c, strip),
            device_id_type=MESH,
        )
        return here, came.at[a], copy

    def pass_on(n):
        def one(at_first):
            here, came, copy = forward_copy(n, at_first)
            pltpu.make_async_copy(here, here, came).wait()
            copy.start()

        if n < len(PASSED[-1]):
            pl.when(q == 0)(lambda: one(True))
        if n < len(PASSED[1]):
            pl.when(q == last)(lambda: one(False))

    def passed_on(n):
        if n < len(PASSED[-1]):
            pl.when(q == 0)(lambda: forward_copy(n, True)[2].wait_send())
        if n < len(PASSED[1]):
            pl.when(q == last)(lambda: forward_copy(n, False)[2].wait_send())

    def tile_sends(act, times=(0, 1)):
        for here in range(2):

            @pl.when(c == here)
            def _():
                for n in range(4):
                    for dq in (-1, 1):
                        j = n // 2 if dq < 0 else 1 - n // 2
                        core = (here + n) % 2

                        far = q == (mid if dq < 0 else mid - 1)

                        def send_parts(relay):
                            for part in (0, 1) if n == 3 else (None,):
                                if relay is None or relay == ((n, part) in PASSED[dq]):
                                    act(tile_copy(dq, j, core, bool(relay), part))

                        for time in times:
                            if dq < 0:
                                if time == 0:
                                    when(has_prev, jnp.logical_not(far))(lambda: send_parts(None))
                                else:
                                    when(far)(lambda: send_parts(False))
                                    when(far)(lambda: send_parts(True))
                            else:
                                waiting = apart if time == 1 else jnp.logical_not(apart)
                                when(has_next, waiting, jnp.logical_not(far))(lambda: send_parts(None))
                                when(far)(lambda: send_parts(time == 1))

    def start(copy):
        copy.start()

    def wait_send(copy):
        copy.wait_send()

    tile_sends(start, (0,))
    swap.start()

    first = lax.broadcasted_iota(jnp.int32, (CELLS, CELLS), 1) * LOOK_RG
    lane = lax.broadcasted_iota(jnp.int32, (CELLS, CELLS), 0)

    def fill(i, carry):
        delta = lane + i * CELLS - first
        inside = jnp.logical_and(delta >= 0, delta < LOOK_RG)
        table[pl.ds(pl.multiple_of(i * CELLS, CELLS), CELLS), :] = jnp.where(inside, 1.0, 0.0).astype(BF16)
        return carry

    lax.fori_loop(0, WIDTH // CELLS, fill, 0)

    @pl.when(jnp.logical_or(apart, jnp.logical_or(q == mid - 1, q == mid)))
    def _():
        pl.semaphore_wait(ready, 2)
        tile_sends(start, (1,))

    row = lax.broadcasted_iota(jnp.int32, (ROWS, ROWS), 0)
    col = lax.broadcasted_iota(jnp.int32, (ROWS, ROWS), 1)
    order = jnp.where(col == LOOK_AZ * (row % LOOKS) + row // LOOKS, 1.0, 0.0).astype(BF16)
    sub = lax.broadcasted_iota(jnp.int32, (LOOKS, CELLS), 0)
    lane8 = lax.broadcasted_iota(jnp.int32, (LOOKS, CELLS), 1)
    left = lane8 < CELLS // 2

    @pl.when(jnp.logical_not(has_up))
    def _():
        edge[0] = jnp.zeros(edge.shape[1:], F32)

    @pl.when(jnp.logical_not(has_down))
    def _():
        edge[1] = jnp.zeros(edge.shape[1:], F32)

    def get_tile(rel, a, part):
        @when(chip_ok(rel))
        def _():
            whole, second_half = (ur, ur2) if rel > 0 else (vr, vr2)
            ref = part_of(tiles.at[1 + rel, a], part)
            pltpu.make_async_copy(ref, ref, (second_half if part == 1 else whole).at[a]).wait()
            reorder(rel, a, part)

    def reorder(rel, a, part):
        at = slice(None) if part is None else pl.ds(part * HALF // 2, HALF // 2)
        for i in range(2):
            looks[1 + rel, a, i, :, at] = jnp.dot(order, tiles[1 + rel, a, i, :, at], preferred_element_type=F32)

    def rims(x):
        d = jnp.where(sub < 3, pltpu.roll(x, 3, 0), 0.0)
        d = d + pltpu.roll(d, LOOKS - 1, 0) + pltpu.roll(d, LOOKS - 2, 0)
        u = jnp.where(jnp.logical_and(sub >= 1, sub < 4), pltpu.roll(x, 1, 0), 0.0)
        u = u + pltpu.roll(u, 1, 0) + pltpu.roll(u, 2, 0)
        return d[0:4], u[0:4]

    def planes_of(stage, own, far):
        planes = list(STAGES[stage]) if own else []
        if far:
            for (pair0, _), (pair1, _) in BACK[stage]:
                planes.append(pair((-1, (pair0[0], pair1[0])), (1, (pair0[1], pair1[1]))))
        return [(kind, (u[0], by_core(u[1])), (v[0], by_core(v[1]))) for kind, u, v in planes]

    def looked(planes, at0, part):
        n = len(planes)
        m = n + n % 2

        def lanes(t, carry):
            at = pl.ds(pl.multiple_of(t * CELLS, CELLS), CELLS)
            at2 = pl.ds(pl.multiple_of(t * CELLS + HALF, CELLS), CELLS)

            def total(x):
                return jnp.sum(x.reshape(LOOK_AZ, LOOKS, CELLS), axis=0)

            for i, (kind, u, v) in enumerate(planes):
                u_r, u_i = looks[1 + u[0], u[1], 0, :, at], looks[1 + u[0], u[1], 1, :, at]
                v_r, v_i = looks[1 + v[0], v[1], 0, :, at], looks[1 + v[0], v[1], 1, :, at]
                if kind == "pair":
                    x, y = u_r * v_r + u_i * v_i, u_i * v_r - u_r * v_i
                else:
                    x, y = u_r * u_r + u_i * u_i, v_r * v_r + v_i * v_i
                sums[at0 + i, :, at] = total(x)
                sums[at0 + i, :, at2] = total(y)
            return carry

        steps = HALF // CELLS
        spans = [(0, WIDTH)]
        first_, end = 0, steps
        if part is not None:
            spans = [(part * HALF // 2, HALF // 2), (HALF + part * HALF // 2, HALF // 2)]
            first_, end = part * steps // 2, (part + 1) * steps // 2
        lax.fori_loop(first_, end, lanes, 0)
        if m > n:
            sums[at0 + n] = jnp.zeros((LOOKS, WIDTH), F32)
        out = None
        for at, width in spans:
            x = sums[at0 : at0 + m, :, at : at + width].reshape(m * LOOKS, width)
            hi = x.astype(BF16)
            lo = (x - hi.astype(F32)).astype(BF16)
            t = table[at : at + width, :]
            both = jnp.dot(jnp.concatenate([hi, lo], axis=0), t, preferred_element_type=F32)
            y = both[0 : m * LOOKS] + both[m * LOOKS :]
            out = y if out is None else out + y
        return out

    def as_planes(out):
        return (out * PLANE_SCALE).reshape(out.shape[0] // LOOKS, LOOKS, CELLS)

    def put_back(places, out):
        for i, place in places:
            place = by_core(place)
            back[place] = out[i]
            back_rim[0, place], back_rim[1, place] = rims(out[i])

    def put_own(stage, out):
        for i in range(len(STAGES[stage])):
            res[c, STARTS[stage] + i] = out[i]
            rim[0, STARTS[stage] + i], rim[1, STARTS[stage] + i] = rims(out[i])
        if stage in BACK_POWER:
            put_back([(2, both) for both in zip(*BACK_POWER[stage], strict=True)], out)

    def put_far(stage, out):
        put_back([(i, (p0, p1)) for i, ((_, p0), (_, p1)) in enumerate(BACK[stage])], out)

    def compute(stage):
        out = as_planes(looked(planes_of(stage, True, True), 0, None))
        put_own(stage, out)
        put_far(stage, out[len(STAGES[stage]) :])

    def span_of(stage, core):
        if stage == 0:
            return pl.ds(0, 8)
        return pl.ds(STARTS[stage] + 2 * core, NEEDS[stage][0][1])

    def core_send(stage):
        return pltpu.make_async_remote_copy(
            src_ref=res.at[c, span_of(stage, other)],
            dst_ref=res.at[c, span_of(stage, other)],
            send_sem=ps.at[stage],
            recv_sem=pr.at[stage],
            device_id=device(0, other, 0),
            device_id_type=MESH,
        )

    def rim_send(stage, core, ds):
        first_, size = NEEDS[stage][core]
        side = (1 - ds) // 2
        span = pl.ds(STARTS[stage] + first_, size)
        return pltpu.make_async_remote_copy(
            src_ref=rim.at[side, span],
            dst_ref=edge.at[side, c, span],
            send_sem=hs.at[stage, core, side],
            recv_sem=hr.at[stage],
            device_id=device(0, core, ds),
            device_id_type=MESH,
        )

    def back_send(m, ds):
        _, _, core, first_, size = BACK_SENDS[m]
        span, there = pl.ds(first_, size), pl.ds(N_OWN + first_, size)
        if ds == 0:
            src, dst = back.at[span], res.at[c, there]
        else:
            side = (1 - ds) // 2
            src, dst = back_rim.at[side, span], edge.at[side, c, there]
        return pltpu.make_async_remote_copy(
            src_ref=src,
            dst_ref=dst,
            send_sem=bs.at[m, 1 + ds],
            recv_sem=br.at[m, 0 if ds == 0 else 1],
            device_id=device(-1, core, ds),
            device_id_type=MESH,
        )

    def back_sends(stage, act):
        for here in range(2):
            specs = [m for m, spec in enumerate(BACK_SENDS) if spec[0] == stage and spec[1] == here]
            if specs:

                @when(c == here, has_prev)
                def _():
                    for ds in (-1, 1, 0):

                        @when(side_ok(ds))
                        def _():
                            for m in specs:
                                act(back_send(m, ds))

    def own_sends(stage, act):
        for ds in (-1, 1):

            @when(side_ok(ds))
            def _():
                for core in range(2):
                    act(rim_send(stage, core, ds))

        act(core_send(stage))

    def all_sends(stage, act):
        back_sends(stage, act)
        own_sends(stage, act)

    def wait_for(ref, sem):
        pltpu.make_async_copy(ref, ref, sem).wait()

    def edge_wait(h, span, sem):
        here = edge if h is None else edge.at[:, pl.ds(h, 1)]
        when(has_up, has_down)(lambda: wait_for(here.at[:, :, span], sem))
        when(jnp.logical_not(has_up))(lambda: wait_for(here.at[1, :, span], sem))
        when(jnp.logical_not(has_down))(lambda: wait_for(here.at[0, :, span], sem))

    def own_arrivals(stage):
        wait_for(res.at[other, span_of(stage, c)], pr.at[stage])
        if stage == 0:
            for core in range(2):
                first_, size = NEEDS[0][core]
                pl.when(c == core)(lambda: edge_wait(None, pl.ds(first_, size), hr.at[0]))
        else:
            edge_wait(None, span_of(stage, c), hr.at[stage])

    def back_arrivals(stage):
        for core in range(2):

            @when(has_next, c == core)
            def _():
                for m, (after, h, to, first_, size) in enumerate(BACK_SENDS):
                    if after == stage and to == core:
                        span = pl.ds(N_OWN + first_, size)
                        wait_for(res.at[h, span], br.at[m, 0])
                        edge_wait(h, span, br.at[m, 1])

    def low(p0, p1):
        return jnp.where(left, p0, pltpu.roll(p1, CELLS // 2, 1))

    def high(p0, p1):
        return jnp.where(left, pltpu.roll(p0, CELLS // 2, 1), p1)

    def rows_box(h, plane):
        x = res[h, plane]
        total = x + jnp.concatenate([edge[0, h, plane], edge[1, h, plane]], axis=0)
        for k in range(1, 4):
            total = total + jnp.where(sub >= k, pltpu.roll(x, k, 0), 0.0)
            total = total + jnp.where(sub < LOOKS - k, pltpu.roll(x, LOOKS - k, 0), 0.0)
        return total

    def cells_box(x):
        total = x
        for k in range(1, 4):
            total = total + jnp.where(lane8 >= k, pltpu.roll(x, k, 1), 0.0)
            total = total + jnp.where(lane8 < CELLS - k, pltpu.roll(x, CELLS - k, 1), 0.0)
        return total

    def ref_boxes():
        for j in range(2):
            r0, r1 = rows_box(0, 5 + j), rows_box(1, 5 + j)
            box_ref[j] = cells_box(jnp.where(c == 0, low(r0, r1), high(r0, r1)))

    def coherences(step):
        for core in range(2):

            @pl.when(c == core)
            def _():
                for j, off, place, sec, half in finals(core, step):
                    p0, p1 = res[0, place[0]], res[1, place[1]]
                    every_ifg[j, off - 1, 0] = low(p0, p1)
                    every_ifg[j, off - 1, 1] = high(p0, p1)
                    b0, b1 = rows_box(0, place[0]), rows_box(1, place[1])
                    s0, s1 = rows_box(0, sec[0]), rows_box(1, sec[1])
                    box_r, box_i = cells_box(low(b0, b1)), cells_box(high(b0, b1))
                    box_s = cells_box(high(s0, s1) if half else low(s0, s1))
                    top = jnp.sqrt(box_r * box_r + box_i * box_i)
                    every_coh[j, off - 1] = top / jnp.sqrt(box_ref[j] * box_s)

    own_copy.wait()
    second_copy.wait()
    count_copy.wait()
    chosen = []
    for j in range(2):
        for slot in range(SLOTS):
            off = jnp.clip(second[j, slot] - (4 * q + 2 * c + j), 1, OFFS)
            chosen.append((j, slot, off - 1, slot < count[j]))
    swap.wait_recv()
    for a in range(4):
        reorder(0, a, None)
    compute(0)
    all_sends(0, start)
    swap.wait_send()
    for stage in range(1, 5):
        b, a = by_core(NEXT[stage - 1]), by_core(PREV[stage - 1])
        if stage < 4:
            get_tile(1, b, None)
            get_tile(-1, a, None)
            compute(stage)
            all_sends(stage, start)
        else:
            own, far = planes_of(4, True, False), planes_of(4, False, True)
            get_tile(1, b, 0)
            own_out = looked(own, 0, 0)
            get_tile(-1, a, 0)
            far_out = looked(far, 6, 0)
            get_tile(1, b, 1)
            put_own(4, as_planes(own_out + looked(own, 0, 1)))
            own_sends(4, start)
            get_tile(-1, a, 1)
            put_far(4, as_planes(far_out + looked(far, 6, 1)))
            back_sends(4, start)
        if stage == 1:
            pass_on(0)
        if stage == 2:
            pass_on(1)
            pass_on(2)
        all_sends(stage - 1, wait_send)
        own_arrivals(stage - 1)
        if stage == 1:
            ref_boxes()
            coherences(0)
        if stage == 3:
            coherences(1)
    tile_sends(wait_send)
    for n in range(3):
        passed_on(n)
    back_arrivals(3)
    coherences(3)
    own_arrivals(4)
    coherences(2)
    all_sends(4, wait_send)
    back_arrivals(4)
    coherences(4)

    zero = jnp.zeros((LOOKS, CELLS), F32)
    for j, slot, off, used in chosen:
        for part in range(2):
            ifg[j, slot, part] = jnp.where(used, every_ifg[j, off, part], zero)
        coh[j, slot] = jnp.where(used, every_coh[j, off], zero)


def store_kernel(ifg, coh, ifg_out, coh_out, sems):
    copies = [
        pltpu.make_async_copy(ifg, ifg_out, sems.at[0]),
        pltpu.make_async_copy(coh, coh_out, sems.at[1]),
    ]
    for copy in copies:
        copy.start()
    for copy in copies:
        copy.wait()


def shards(slc, pair_second, pair_count):
    dma = pltpu.SemaphoreType.DMA
    hbm = pl.BlockSpec(memory_space=pltpu.HBM)
    vmem = pl.BlockSpec(memory_space=pltpu.VMEM)
    ifg_shape = (2, SLOTS, 2, LOOKS, CELLS)
    coh_shape = (2, SLOTS, LOOKS, CELLS)
    operands = [pltpu.with_memory_space_constraint(x, pltpu.HBM) for x in (slc, pair_second, pair_count)]
    ifg, coh = pl.pallas_call(
        planes_kernel,
        out_shape=(pltpu.VMEM(ifg_shape, F32), pltpu.VMEM(coh_shape, F32)),
        in_specs=[hbm, hbm, hbm],
        out_specs=(vmem, vmem),
        scratch_shapes=[
            pltpu.VMEM((2, N_PLANES, LOOKS, CELLS), F32),
            pltpu.VMEM((2, 2, N_PLANES, 4, CELLS), F32),
            pltpu.VMEM((3, 4, 2, ROWS, HALF), BF16),
            pltpu.VMEM((3, 4, 2, ROWS, HALF), F32),
            pltpu.VMEM((10, LOOKS, WIDTH), F32),
            pltpu.VMEM((WIDTH, CELLS), BF16),
            pltpu.VMEM((N_BACK, LOOKS, CELLS), F32),
            pltpu.VMEM((2, N_OWN, 4, CELLS), F32),
            pltpu.VMEM((2, N_BACK, 4, CELLS), F32),
            pltpu.SMEM((2, SLOTS), jnp.int32),
            pltpu.SMEM((2,), jnp.int32),
            pltpu.VMEM((2, OFFS, 2, LOOKS, CELLS), F32),
            pltpu.VMEM((2, OFFS, LOOKS, CELLS), F32),
            pltpu.VMEM((2, LOOKS, CELLS), F32),
            pltpu.SemaphoreType.REGULAR,
            dma,
            dma((2,)),
            dma,
            dma,
            dma((2, 2)),
            dma((4,)),
            dma((2, 2)),
            dma((4,)),
            dma,
            dma((4,)),
            dma,
            dma((4,)),
            dma((3,)),
            dma((5,)),
            dma((5,)),
            dma((5, 2, 2)),
            dma((5,)),
            dma((8, 3)),
            dma((8, 2)),
        ],
        compiler_params=pltpu.CompilerParams(
            collective_id=0, has_side_effects=True, vmem_limit_bytes=40 * 2**20
        ),
    )(*operands)
    return pl.pallas_call(
        store_kernel,
        out_shape=(jax.ShapeDtypeStruct(ifg_shape, F32), jax.ShapeDtypeStruct(coh_shape, F32)),
        in_specs=[vmem, vmem],
        out_specs=(pl.BlockSpec(memory_space=pl.ANY), pl.BlockSpec(memory_space=pl.ANY)),
        scratch_shapes=[dma((2,))],
        compiler_params=pltpu.CompilerParams(vmem_limit_bytes=16 * 2**20),
    )(ifg, coh)


def solution(mesh):
    in_specs = (P("date", None, "strip", None), P("date", None), P("date"))
    out_specs = (P("date", None, None, "strip", None), P("date", None, "strip", None))
    return jax.shard_map(shards, mesh=mesh, in_specs=in_specs, out_specs=out_specs, check_vma=False)
```
